32 devices in a mesh: gx: 8 (over z, core), gy: 4 (over y, x).
Axes of the slice: x: 2, y: 2, z: 4, core: 2. Of those that a mesh axis runs over, the one named last changes fastest.
Arguments:
- field: bfloat16 [64, 32, 16, 256], P(None, 'gx', 'gy'), may hold values from -6 to 6
- weight_first: bfloat16 [64, 1728], replicated, may hold values from -0.15625 to 0.15625
- weight_down: bfloat16 [128, 512], replicated, may hold values from -0.25 to 0.25
- weight_coarse: bfloat16 [128, 3456], replicated, may hold values from -0.109375 to 0.109375
- weight_up: bfloat16 [64, 1024], replicated, may hold values from -0.5 to 0.5
- weight_last: bfloat16 [64, 1728], replicated, may hold values from -0.15625 to 0.15625
- cotangent: bfloat16 [64, 32, 16, 256], P(None, 'gx', 'gy'), may hold values from -0.016479492 to 0.016479492
Outputs:
- output: bfloat16 [64, 32, 16, 256], P(None, 'gx', 'gy')
- grad_first: float32 [64, 1728], replicated
- grad_down: float32 [128, 512], replicated
- grad_coarse: float32 [128, 3456], replicated
- grad_up: float32 [64, 1024], replicated
- grad_last: float32 [64, 1728], replicated
The draws below stay inside these ranges and needn't reach their ends.
All inputs are finite; a program needn't handle non-finite values.
Results may differ from the reference program's by a relative error of at most 0.0069.
Values may be sent and summed in bfloat16 or wider, within the bound.
A program may use at most 128 MiB of HBM per device.

```python
import jax
import jax.numpy as jnp

CX = 4
CY = 4
CZ = 256
C1 = 64
C2 = 128
NX = 32
NY = 16
N_GX = 8
N_GY = 4


def levels(own_key, extent, split, low, largest):
    level = 1.0
    for axis_at, shards_of in split:
        steps = jax.random.uniform(jax.random.fold_in(jax.random.fold_in(own_key, 6), axis_at), (shards_of,), jnp.float32, low / len(split), largest / len(split))
        level = level * jnp.repeat(jnp.exp(steps), extent[axis_at] // shards_of).reshape((-1,) + (1,) * (len(extent) - 1 - axis_at))
    return level


def normal_values(own_key, dims, width, limit, cuts=(), held_as=jnp.bfloat16):
    values = jax.random.normal(own_key, dims, jnp.float32) * width
    if len(cuts) > 0:
        values = levels(own_key, dims, cuts, -0.22, 0.18) * values
    return jnp.clip(values, min=-limit, max=limit).astype(held_as)


def setup_inputs(seed: int = 0) -> dict:
    key_list = jax.random.split(jax.random.key(seed), 8)
    return {
        "field": normal_values(key_list[0], (C1, NX, NY, CZ), 1.0, 6.0, ((1, 8), (2, 4))),
        "weight_first": normal_values(key_list[1], (C1, 27 * C1), (27 * C1) ** -0.5, 0.15625),
        "weight_down": normal_values(key_list[2], (C2, 8 * C1), (8 * C1) ** -0.5, 0.25),
        "weight_coarse": normal_values(key_list[3], (C2, 27 * C2), (27 * C2) ** -0.5, 0.109375),
        "weight_up": normal_values(key_list[4], (C1, 8 * C2), C2 ** -0.5, 0.5),
        "weight_last": normal_values(key_list[5], (C1, 27 * C1), (27 * C1) ** -0.5, 0.15625),
        "cotangent": normal_values(key_list[6], (C1, NX, NY, CZ), (1.0 / (CX * CY * CZ * N_GX * N_GY) ** 0.5), 0.016479492, ((1, 8), (2, 4))),
    }


def leaky(values):
    return 0.505 * values + 0.495 * (jnp.sqrt(values * values + 1.0) - 1.0)

def slope_of(values):
    values = values.astype(jnp.float32)
    return 0.505 + 0.495 * values / jnp.sqrt(values * values + 1.0)

def pad_plane(volume):
    return jnp.pad(volume, ((0, 0), (1, 1), (1, 1), (0, 0)))

def convolve(padded, weight, flipped):
    padded = padded.astype(jnp.float32)
    taps = weight.astype(jnp.float32).reshape(weight.shape[0], 27, -1)
    zpadded = jnp.pad(padded, ((0, 0), (0, 0), (0, 0), (1, 1)))
    size_x = padded.shape[1] - 2
    size_y = padded.shape[2] - 2
    size_z = padded.shape[3]
    total = None
    for along_x in range(3):
        for along_y in range(3):
            for along_z in range(3):
                window = zpadded[:, along_x:along_x + size_x, along_y:along_y + size_y, along_z:along_z + size_z]
                if flipped:
                    tap_index = (2 - along_x) * 9 + (2 - along_y) * 3 + (2 - along_z)
                    term = jnp.einsum('oi,oxyz->ixyz', taps[:, tap_index], window)
                else:
                    tap_index = along_x * 9 + along_y * 3 + along_z
                    term = jnp.einsum('oi,ixyz->oxyz', taps[:, tap_index], window)
                total = term if total is None else total + term
    return total

def conv_grad(cotan, padded):
    cotan = cotan.astype(jnp.float32)
    zpadded = jnp.pad(padded.astype(jnp.float32), ((0, 0), (0, 0), (0, 0), (1, 1)))
    size_x, size_y, size_z = (cotan.shape[1], cotan.shape[2], cotan.shape[3])
    pieces = []
    for along_x in range(3):
        for along_y in range(3):
            for along_z in range(3):
                window = zpadded[:, along_x:along_x + size_x, along_y:along_y + size_y, along_z:along_z + size_z]
                pieces.append(jnp.einsum('oxyz,ixyz->oi', cotan, window))
    return jnp.stack(pieces, axis=1).reshape(cotan.shape[0], -1)

def shrink(fine, weight, transposed):
    fine = fine.astype(jnp.float32)
    taps = weight.astype(jnp.float32).reshape(weight.shape[0], 8, -1)
    total = None
    for half_x in range(2):
        for half_y in range(2):
            for half_z in range(2):
                tap_index = half_x * 4 + half_y * 2 + half_z
                window = fine[:, half_x::2, half_y::2, half_z::2]
                if transposed:
                    term = jnp.einsum('oi,oxyz->ixyz', taps[:, tap_index], window)
                else:
                    term = jnp.einsum('oi,ixyz->oxyz', taps[:, tap_index], window)
                total = term if total is None else total + term
    return total

def spread(source, weight, transposed):
    source = source.astype(jnp.float32)
    taps = weight.astype(jnp.float32).reshape(weight.shape[0], 8, -1)
    channels = taps.shape[2] if transposed else taps.shape[0]
    size_x, size_y, size_z = (source.shape[1], source.shape[2], source.shape[3])
    result = jnp.zeros((channels, 2 * size_x, 2 * size_y, 2 * size_z), jnp.float32)
    for half_x in range(2):
        for half_y in range(2):
            for half_z in range(2):
                tap_index = half_x * 4 + half_y * 2 + half_z
                if transposed:
                    term = jnp.einsum('oi,oxyz->ixyz', taps[:, tap_index], source)
                else:
                    term = jnp.einsum('oi,ixyz->oxyz', taps[:, tap_index], source)
                result = result.at[:, half_x::2, half_y::2, half_z::2].set(term)
    return result

def pair_grad(outer, inner, outer_fine):
    outer = outer.astype(jnp.float32)
    inner = inner.astype(jnp.float32)
    pieces = []
    for half_x in range(2):
        for half_y in range(2):
            for half_z in range(2):
                if outer_fine:
                    pieces.append(jnp.einsum('oxyz,ixyz->oi', outer[:, half_x::2, half_y::2, half_z::2], inner))
                else:
                    pieces.append(jnp.einsum('oxyz,ixyz->oi', outer, inner[:, half_x::2, half_y::2, half_z::2]))
    return jnp.stack(pieces, axis=1).reshape(outer.shape[0], -1)

def reference(field, weight_first, weight_down, weight_coarse, weight_up, weight_last, cotangent):
    hidden = leaky(convolve(pad_plane(field), weight_first, False)).astype(jnp.bfloat16)
    coarse = leaky(shrink(hidden, weight_down, False)).astype(jnp.bfloat16)
    level = leaky(convolve(pad_plane(coarse), weight_coarse, False)).astype(jnp.bfloat16)
    raised = spread(level, weight_up, False)
    summed = (leaky(raised) + hidden.astype(jnp.float32)).astype(jnp.bfloat16)
    output = convolve(pad_plane(summed), weight_last, False).astype(jnp.bfloat16)
    grad_last = conv_grad(cotangent, pad_plane(summed))
    back_sum = convolve(pad_plane(cotangent), weight_last, True)
    back_raised = (back_sum * slope_of(raised)).astype(jnp.bfloat16)
    grad_up = pair_grad(back_raised, level, True)
    back_level = (shrink(back_raised, weight_up, True) * slope_of(level)).astype(jnp.bfloat16)
    grad_coarse = conv_grad(back_level, pad_plane(coarse))
    back_coarse = (convolve(pad_plane(back_level), weight_coarse, True) * slope_of(coarse)).astype(jnp.bfloat16)
    grad_down = pair_grad(back_coarse, hidden, False)
    back_hidden = back_sum + spread(back_coarse, weight_down, True)
    back_first = (back_hidden * slope_of(hidden)).astype(jnp.bfloat16)
    grad_first = conv_grad(back_first, pad_plane(field))
    return (output, grad_first, grad_down, grad_coarse, grad_up, grad_last)
```

```python
import functools

import jax
import jax.numpy as jnp
from jax import lax
from jax.experimental import pallas as pl
from jax.experimental.pallas import tpu as pltpu
from jax.sharding import PartitionSpec as P

MESH = pl.DeviceIdType.MESH
BF16 = jnp.bfloat16
F32 = jnp.float32
VMEM_BYTES = 56 * 1024 * 1024
LANES = 128


def leaky(values):
    return 0.505 * values + 0.495 * (jnp.sqrt(values * values + 1.0) - 1.0)


def slope_of(values):
    values = values.astype(F32)
    return 0.505 + 0.495 * values * lax.rsqrt(values * values + 1.0)


def dot(left, right):
    return jnp.dot(left, right, preferred_element_type=F32)


def dot_nt(left, right):
    return lax.dot_general(left, right, (((1,), (1,)), ((), ())), preferred_element_type=F32)


def call(kernel, args, outs, scratch, name, collective=None):
    params = dict(vmem_limit_bytes=VMEM_BYTES)
    if collective is not None:
        params.update(collective_id=collective, has_side_effects=True)
    return pl.pallas_call(
        kernel,
        out_shape=outs,
        in_specs=[pl.BlockSpec(memory_space=pltpu.VMEM)] * len(args),
        out_specs=[pl.BlockSpec(memory_space=pltpu.VMEM)] * len(outs),
        scratch_shapes=scratch,
        compiler_params=pltpu.CompilerParams(**params),
        name=name,
    )(*args)


def halo_kernel(sizes, counts, *refs):
    number = len(sizes)
    ins, outs, (send, recv) = refs[:number], refs[number : 2 * number], refs[2 * number :]
    n_x, n_y = counts
    me_x, me_y = lax.axis_index("gx"), lax.axis_index("gy")
    steps = [(i, j) for i in (-1, 0, 1) for j in (-1, 0, 1) if (i, j) != (0, 0)]

    def inside(step_x, step_y):
        at_x, at_y = me_x + step_x, me_y + step_y
        return (at_x >= 0) & (at_x < n_x) & (at_y >= 0) & (at_y < n_y)

    def place(step_x, step_y):
        return (
            jnp.clip(me_x + step_x, 0, n_x - 1),
            jnp.clip(me_y + step_y, 0, n_y - 1),
        )

    barrier = pltpu.get_barrier_semaphore()
    for step in steps:

        @pl.when(inside(*step))
        def _(step=step):
            pl.semaphore_signal(barrier, inc=1, device_id=place(*step), device_id_type=MESH)

    pl.semaphore_wait(barrier, sum(inside(*step).astype(jnp.int32) for step in steps))

    def spans(step, extent, width):
        if step == 0:
            return pl.ds(0, extent), pl.ds(width, extent)
        if step > 0:
            return pl.ds(extent - width, width), pl.ds(0, width)
        return pl.ds(0, width), pl.ds(width + extent, width)

    copies = []
    for at, (step_x, step_y) in enumerate(steps):
        for which, (row_width, lane_width) in enumerate(sizes):
            rows, lanes = ins[which].shape
            row_from, row_to = spans(step_y, rows, row_width)
            lane_from, lane_to = spans(step_x, lanes, lane_width)
            copies.append(
                (
                    step_x,
                    step_y,
                    pltpu.make_async_remote_copy(
                        src_ref=ins[which].at[row_from, lane_from],
                        dst_ref=outs[which].at[row_to, lane_to],
                        send_sem=send.at[at, which],
                        recv_sem=recv.at[at, which],
                        device_id=place(step_x, step_y),
                        device_id_type=MESH,
                    ),
                )
            )
    for step_x, step_y, copy in copies:

        @pl.when(inside(step_x, step_y))
        def _(copy=copy):
            copy.start()

    for which, (row_width, lane_width) in enumerate(sizes):
        rows, lanes = ins[which].shape
        outs[which][row_width : row_width + rows, lane_width : lane_width + lanes] = ins[which][...]
        for step_x, step_y in steps:
            row_at = {-1: (0, row_width), 0: (row_width, rows), 1: (row_width + rows, row_width)}[step_y]
            lane_at = {-1: (0, lane_width), 0: (lane_width, lanes), 1: (lane_width + lanes, lane_width)}[step_x]

            @pl.when(jnp.logical_not(inside(step_x, step_y)))
            def _(row_at=row_at, lane_at=lane_at, which=which):
                outs[which][
                    row_at[0] : row_at[0] + row_at[1], lane_at[0] : lane_at[0] + lane_at[1]
                ] = jnp.zeros((row_at[1], lane_at[1]), BF16)

    for step_x, step_y, copy in copies:

        @pl.when(inside(-step_x, -step_y))
        def _(copy=copy):
            copy.wait_recv()

    for step_x, step_y, copy in copies:

        @pl.when(inside(step_x, step_y))
        def _(copy=copy):
            copy.wait_send()


def halo(blocks, sizes, counts, collective):
    outs = [
        jax.ShapeDtypeStruct((b.shape[0] + 2 * r, b.shape[1] + 2 * l), b.dtype)
        for b, (r, l) in zip(blocks, sizes)
    ]
    scratch = [pltpu.SemaphoreType.DMA((8, len(sizes))), pltpu.SemaphoreType.DMA((8, len(sizes)))]
    return call(
        functools.partial(halo_kernel, sizes, counts),
        blocks, outs, scratch, "halo%d" % collective, collective,
    )


def sum_kernel(chunk, counts, x_ref, full, r1, s1, r2, s2, r3, send, recv):
    n_x, n_y = counts
    n_z = n_x // 2
    me_x, me_y = lax.axis_index("gx"), lax.axis_index("gy")
    core, me_z = lax.rem(me_x, 2), me_x // 2
    mid, half = chunk * n_z, chunk * n_z * n_y
    twin = (me_z * 2 + 1 - core, me_y)

    def y_peer(step):
        return lax.rem(me_y + step, n_y)

    def z_peer(step):
        return lax.rem(me_z + step, n_z)

    def y_place(step):
        return (me_x, y_peer(step))

    def z_place(step):
        return (z_peer(step) * 2 + core, me_y)

    barrier = pltpu.get_barrier_semaphore()
    peers = [twin] + [y_place(k) for k in range(1, n_y)] + [z_place(k) for k in range(1, n_z)]
    for peer in peers:
        pl.semaphore_signal(barrier, inc=1, device_id=peer, device_id_type=MESH)
    pl.semaphore_wait(barrier, len(peers))

    def copy(src, dst, at, place):
        made = pltpu.make_async_remote_copy(
            src_ref=src, dst_ref=dst, send_sem=send.at[at], recv_sem=recv.at[at],
            device_id=place, device_id_type=MESH,
        )
        made.start()
        return made

    def rows(start, size):
        return pl.ds(pl.multiple_of(start, 16), size)

    started = []
    count = 0
    mine = core * half
    one = copy(x_ref.at[rows((1 - core) * half, half)], r1, 0, twin)
    one.wait_recv()
    started.append(one)
    s1[...] = (x_ref[rows(mine, half), :].astype(F32) + r1[...].astype(F32)).astype(BF16)
    count = 1
    group = []
    for k in range(1, n_y):
        group.append(copy(s1.at[rows(y_peer(k) * mid, mid)], r2.at[k - 1], count, y_place(k)))
        count += 1
    total = s1[rows(me_y * mid, mid), :].astype(F32)
    for k, made in enumerate(group):
        made.wait_recv()
        total = total + r2[k].astype(F32)
    s2[...] = total.astype(BF16)
    started += group
    group = []
    for k in range(1, n_z):
        group.append(copy(s2.at[rows(z_peer(k) * chunk, chunk)], r3.at[k - 1], count, z_place(k)))
        count += 1
    total = s2[rows(me_z * chunk, chunk), :].astype(F32)
    for k, made in enumerate(group):
        made.wait_recv()
        total = total + r3[k].astype(F32)
    started += group
    base = mine + me_y * mid
    own = rows(base + me_z * chunk, chunk)
    full[own, :] = total.astype(BF16)
    group = []
    for k in range(1, n_z):
        group.append(copy(full.at[own], full.at[own], count, z_place(k)))
        count += 1
    for made in group:
        made.wait_recv()
    started += group
    own = rows(base, mid)
    group = []
    for k in range(1, n_y):
        group.append(copy(full.at[own], full.at[own], count, y_place(k)))
        count += 1
    for made in group:
        made.wait_recv()
    started += group
    own = rows(mine, half)
    last = copy(full.at[own], full.at[own], count, twin)
    last.wait_recv()
    started.append(last)
    for made in started:
        made.wait_send()


def sum_all(packed, chunk, counts, collective):
    n_x, n_y = counts
    n_z = n_x // 2
    copies = 2 + 2 * (n_y - 1) + 2 * (n_z - 1)
    half, mid = chunk * n_z * n_y, chunk * n_z
    scratch = [
        pltpu.VMEM((half, LANES), BF16),
        pltpu.VMEM((half, LANES), BF16),
        pltpu.VMEM((max(n_y - 1, 1), mid, LANES), BF16),
        pltpu.VMEM((mid, LANES), BF16),
        pltpu.VMEM((max(n_z - 1, 1), chunk, LANES), BF16),
        pltpu.SemaphoreType.DMA((copies,)),
        pltpu.SemaphoreType.DMA((copies,)),
    ]
    return call(
        functools.partial(sum_kernel, chunk, counts),
        [packed], [jax.ShapeDtypeStruct(packed.shape, BF16)], scratch, "sum_all", collective,
    )[0]


def parity_matrix(size, inverse):
    first = lax.broadcasted_iota(jnp.int32, (size, size), 0)
    second = lax.broadcasted_iota(jnp.int32, (size, size), 1)
    if inverse:
        first, second = second, first
    half = size // 2
    wanted = jnp.where(second < half, 2 * second, 2 * (second - half) + 1)
    return jnp.where(first == wanted, 1.0, 0.0).astype(BF16)


def moved(block, forward):
    lanes = block.shape[1]
    at = lax.broadcasted_iota(jnp.int32, block.shape, 1)
    turned = pltpu.roll(block.astype(F32), 1 if forward else lanes - 1, 1)
    return jnp.where(at == (0 if forward else lanes - 1), 0.0, turned).astype(BF16)


def fine_shifts(source, target):
    rows, lanes = source.shape
    half = LANES
    size = 2 * half
    def step(x, _):
        base = pl.multiple_of(x * size, size)
        even = source[:, pl.ds(base, half)]
        odd = source[:, pl.ds(base + half, half)]
        target[0:rows, pl.ds(base, half)] = moved(odd, True)
        target[0:rows, pl.ds(base + half, half)] = even
        target[rows : 2 * rows, pl.ds(base, half)] = even
        target[rows : 2 * rows, pl.ds(base + half, half)] = odd
        target[2 * rows : 3 * rows, pl.ds(base, half)] = odd
        target[2 * rows : 3 * rows, pl.ds(base + half, half)] = moved(even, False)
        return 0
    lax.fori_loop(0, lanes // size, step, 0)


def coarse_shifts(source, target):
    rows, lanes = source.shape
    for x in range(lanes // LANES):
        block = source[:, x * LANES : (x + 1) * LANES]
        target[0:rows, x * LANES : (x + 1) * LANES] = moved(block, True)
        target[rows : 2 * rows, x * LANES : (x + 1) * LANES] = block
        target[2 * rows : 3 * rows, x * LANES : (x + 1) * LANES] = moved(block, False)


def fine_conv(shifted, weight, store):
    size = 2 * LANES
    def step(x, _):
        total = None
        for along_x in range(3):
            base = pl.multiple_of((x + along_x) * size, size)
            term = dot(weight[along_x], shifted[:, pl.ds(base, size)])
            total = term if total is None else total + term
        store(pl.ds(pl.multiple_of(x * size, size), size), total)
        return 0
    lax.fori_loop(0, shifted.shape[1] // size - 2, step, 0)


def coarse_conv(shifted, weight):
    width = shifted.shape[1] - 2 * LANES
    total = None
    for along_x in range(3):
        term = dot(weight[along_x], shifted[:, along_x * LANES : along_x * LANES + width])
        total = term if total is None else total + term
    return total


def cells(n_qx, n_qy):
    found = []
    for a in range(2):
        for c in range(2):
            for qy in range(n_qy):
                for qx in range(n_qx):
                    found.append((2 * a + c, qy * n_qx + qx, qy, (2 * qx + a) * 2 + c))
    return found


def part(row, lane):
    return (slice(row * LANES, (row + 1) * LANES), slice(lane * LANES, (lane + 1) * LANES))


def to_wide(value, n_qy, channels):
    return jnp.concatenate([value[q * channels : (q + 1) * channels] for q in range(n_qy)], axis=1)


def first_kernel(field, cotan, w_first, w_last_t, w_down, hidden, coarse, back_sum, field_z, cotan_z, work, cells_ref, shifted):
    size = 2 * LANES
    matrix = parity_matrix(size, False)
    blocks = field.shape[1] // size
    for x in range(blocks):
        field_z[:, x * size : (x + 1) * size] = dot(field[:, x * size : (x + 1) * size], matrix).astype(BF16)
        work[:, x * size : (x + 1) * size] = dot(cotan[:, x * size : (x + 1) * size], matrix).astype(BF16)
    fine_shifts(field_z, shifted)

    def store_hidden(where, value):
        hidden[:, where] = leaky(value).astype(BF16)

    fine_conv(shifted, w_first, store_hidden)
    n_qx, n_qy = (blocks - 2) // 2, hidden.shape[0] // LANES
    for row, lane, fine_row, fine_lane in cells(n_qx, n_qy):
        cells_ref[part(row, lane)] = hidden[part(fine_row, fine_lane)]
    value = leaky(dot(w_down[...], cells_ref[...])).astype(BF16)
    width = n_qx * LANES
    for qy in range(n_qy):
        coarse[qy * LANES : (qy + 1) * LANES, :] = value[:, qy * width : (qy + 1) * width]
    rim = (work.shape[0] - hidden.shape[0]) // 2
    cotan_z[...] = work[rim : rim + hidden.shape[0], size : size + hidden.shape[1]]
    fine_shifts(work, shifted)

    def store_back(where, value):
        back_sum[:, where] = value

    fine_conv(shifted, w_last_t, store_back)


def level_kernel(coarse, w_coarse, w_up, w_up_t, hidden, back_sum, summed, back_level, grad_up, raised, back_cells, shifted):
    coarse_shifts(coarse, shifted)
    n_qx, n_qy = coarse.shape[1] // LANES - 2, coarse.shape[0] // LANES - 2
    level = to_wide(leaky(coarse_conv(shifted, w_coarse)).astype(BF16), n_qy, LANES)
    raised[...] = dot(w_up[...], level)
    for row, lane, fine_row, fine_lane in cells(n_qx, n_qy):
        here, fine = part(row, lane), part(fine_row, fine_lane)
        value = raised[here]
        root = lax.rsqrt(value * value + 1.0)
        summed[fine] = (leaky(value) + hidden[fine].astype(F32)).astype(BF16)
        back_cells[here] = (back_sum[fine] * (0.505 + 0.495 * value * root)).astype(BF16)
    grad_up[...] = dot_nt(back_cells[...], level)
    back = (dot(w_up_t[...], back_cells[...]) * slope_of(level)).astype(BF16)
    width = n_qx * LANES
    for qy in range(n_qy):
        back_level[qy * LANES : (qy + 1) * LANES, :] = back[:, qy * width : (qy + 1) * width]


def last_kernel(summed, back_level, coarse, hidden, back_sum, field_z, cotan_z, grad_up, w_last, w_coarse_t, w_down_t, output, packed, shifted, shifted_c, back_first, cells_ref, spread, total_ref):
    size = 2 * LANES
    matrix = parity_matrix(size, True)
    packed[...] = jnp.zeros(packed.shape, BF16)
    channels = 64
    n_y = hidden.shape[0] // channels
    n_qx, n_qy = coarse.shape[1] // LANES - 2, coarse.shape[0] // LANES - 2
    width = n_qx * LANES
    fine_rows = summed.shape[0]
    coarse_rows = coarse.shape[0]
    lanes = hidden.shape[1]
    in_half = lax.broadcasted_iota(jnp.int32, (channels, LANES), 1) < channels

    coarse_shifts(back_level, shifted_c)
    center = coarse[LANES : LANES * (1 + n_qy), LANES : LANES + width]
    back = (coarse_conv(shifted_c, w_coarse_t) * slope_of(center)).astype(BF16)
    back_wide = to_wide(back, n_qy, LANES)
    spread[...] = dot(w_down_t[...], back_wide)
    for row, lane, fine_row, fine_lane in cells(n_qx, n_qy):
        here, fine = part(row, lane), part(fine_row, fine_lane)
        mine = hidden[fine]
        cells_ref[here] = mine
        back_first[fine] = ((back_sum[fine] + spread[here]) * slope_of(mine)).astype(BF16)

    base = 27 * channels
    coarse_shifts(coarse, shifted_c)
    center = back_level[LANES : LANES * (1 + n_qy), LANES : LANES + width]
    for along_x in range(3):
        total_ref[:, : 3 * coarse_rows] = dot_nt(center, shifted_c[:, along_x * LANES : along_x * LANES + width])
        for along_z in range(3):
            for along_y in range(3):
                term = None
                for qy in range(n_qy):
                    lane = along_z * coarse_rows + (qy + along_y) * LANES
                    here = total_ref[qy * LANES : (qy + 1) * LANES, lane : lane + LANES]
                    term = here if term is None else term + here
                at = base + (along_x * 9 + along_y * 3 + along_z) * LANES
                packed[at : at + LANES, :] = term.astype(BF16)
    base = base + 27 * LANES
    for k in range(8):
        packed[base + k * 64 : base + k * 64 + 64, :] = grad_up[k * 64 : k * 64 + 64, :].astype(BF16)
    base = base + 512
    down = dot_nt(back_wide, cells_ref[...])
    for k in range(4):
        packed[base + k * LANES : base + (k + 1) * LANES, :] = down[:, k * LANES : (k + 1) * LANES].astype(BF16)

    def weight_grad(left, second):
        for along_x in range(3):
            total_ref[:, : 3 * fine_rows] = dot_nt(left[...], shifted[:, along_x * size : along_x * size + lanes])
            for along_z in range(3):
                total = None
                for y in range(n_y):
                    term = total_ref[y * channels : (y + 1) * channels, along_z * fine_rows : (along_z + 1) * fine_rows]
                    if y > 0:
                        term = pltpu.roll(term, fine_rows - channels * y, 1)
                    term = term[:, : 2 * LANES]
                    total = term if total is None else total + term
                at = (along_x * 3 + along_z) * 3 * channels
                tail = at + 2 * channels
                head = total[:, :LANES].astype(BF16)
                rest = total[:, LANES:]
                if second:
                    packed[at + channels : at + 2 * channels, :] = head
                    rest = pltpu.roll(rest, channels, 1)
                    packed[tail : tail + channels, :] = jnp.where(
                        in_half, packed[tail : tail + channels, :].astype(F32), rest
                    ).astype(BF16)
                else:
                    packed[at : at + channels, :] = head
                    packed[tail : tail + channels, :] = rest.astype(BF16)

    fine_shifts(field_z, shifted)
    weight_grad(back_first, False)
    fine_shifts(summed, shifted)
    weight_grad(cotan_z, True)

    def store(where, value):
        output[:, where] = dot(value.astype(BF16), matrix).astype(BF16)

    fine_conv(shifted, w_last, store)


def banded(weight, n_y, flipped):
    outer = weight.shape[0]
    taps = weight.reshape(outer, 3, 3, 3, -1)
    if flipped:
        taps = jnp.transpose(taps[:, ::-1, ::-1, ::-1], (1, 4, 3, 2, 0))
    else:
        taps = jnp.transpose(taps, (1, 0, 3, 2, 4))
    inner = taps.shape[-1]
    taps = taps.reshape(3, taps.shape[1], 3, 3 * inner)
    bands = [
        jnp.pad(taps, ((0, 0), (0, 0), (0, 0), (y * inner, (n_y - 1 - y) * inner)))
        for y in range(n_y)
    ]
    return jnp.stack(bands, axis=1).reshape(3, n_y * taps.shape[1], 3 * (n_y + 2) * inner)


def shards(counts, field, weight_first, weight_down, weight_coarse, weight_up, weight_last, cotangent):
    channels, size_x, size_y, size_z = field.shape
    wide = weight_down.shape[0]
    n_qx, n_qy = size_x // 2, size_y // 2
    rows, lanes = size_y * channels, size_x * size_z
    fine = lambda v: jnp.transpose(v, (2, 0, 1, 3)).reshape(rows, lanes)
    shape = jax.ShapeDtypeStruct

    w_first = banded(weight_first, size_y, False)
    w_last = banded(weight_last, size_y, False)
    w_last_t = banded(weight_last, size_y, True)
    w_coarse = banded(weight_coarse, n_qy, False)
    w_coarse_t = banded(weight_coarse, n_qy, True)
    w_down = jnp.transpose(weight_down.reshape(wide, 2, 2, 2, channels), (0, 1, 3, 2, 4)).reshape(wide, 8 * channels)
    w_up = jnp.transpose(weight_up.reshape(channels, 2, 2, 2, wide), (1, 3, 2, 0, 4)).reshape(8 * channels, wide)

    fine_rim, coarse_rim = (channels, size_z), (wide, size_z // 2)
    field_w, cotan_w = halo([fine(field), fine(cotangent)], [fine_rim, fine_rim], counts, 0)
    full_rows, full_lanes = field_w.shape
    n_cells = n_qx * n_qy * LANES
    hidden, coarse, back_sum, field_z, cotan_z = call(
        first_kernel,
        [field_w, cotan_w, w_first, w_last_t, w_down],
        [
            shape((rows, lanes), BF16),
            shape((n_qy * wide, n_qx * LANES), BF16),
            shape((rows, lanes), F32),
            shape((full_rows, full_lanes), BF16),
            shape((rows, lanes), BF16),
        ],
        [
            pltpu.VMEM((full_rows, full_lanes), BF16),
            pltpu.VMEM((8 * channels, n_cells), BF16),
            pltpu.VMEM((3 * full_rows, full_lanes), BF16),
        ],
        "first",
    )
    (coarse_w,) = halo([coarse], [coarse_rim], counts, 1)
    coarse_rows, coarse_lanes = coarse_w.shape
    summed, back_level, grad_up = call(
        level_kernel,
        [coarse_w, w_coarse, w_up, w_up.T, hidden, back_sum],
        [
            shape((rows, lanes), BF16),
            shape((n_qy * wide, n_qx * LANES), BF16),
            shape((8 * channels, wide), F32),
        ],
        [
            pltpu.VMEM((8 * channels, n_cells), F32),
            pltpu.VMEM((8 * channels, n_cells), BF16),
            pltpu.VMEM((3 * coarse_rows, coarse_lanes), BF16),
        ],
        "level",
    )
    summed_w, back_level_w = halo([summed, back_level], [fine_rim, coarse_rim], counts, 2)
    used = 27 * channels + 27 * wide + 8 * channels + 4 * wide
    devices = counts[0] * counts[1]
    chunk = -(-used // (devices * 16)) * 16
    output, packed = call(
        last_kernel,
        [summed_w, back_level_w, coarse_w, hidden, back_sum, field_z, cotan_z, grad_up, w_last, w_coarse_t, w_down.T],
        [shape((rows, lanes), BF16), shape((chunk * devices, LANES), BF16)],
        [
            pltpu.VMEM((3 * full_rows, full_lanes), BF16),
            pltpu.VMEM((3 * coarse_rows, coarse_lanes), BF16),
            pltpu.VMEM((rows, lanes), BF16),
            pltpu.VMEM((8 * channels, n_cells), BF16),
            pltpu.VMEM((8 * channels, n_cells), F32),
            pltpu.VMEM((max(rows, n_qy * wide), 3 * max(full_rows, coarse_rows)), F32),
        ],
        "last",
    )
    sums = sum_all(packed, chunk, counts, 3).astype(F32)
    at = 27 * channels
    both = sums[:at].reshape(3, 3, 3, channels, LANES)

    def fine_grad(head, tail):
        units = jnp.concatenate([head, tail], axis=-1).reshape(3, 3, channels, 3, channels)
        return jnp.transpose(units, (2, 0, 3, 1, 4)).reshape(channels, 27 * channels)

    grad_first = fine_grad(both[:, :, 0], both[:, :, 2, :, :channels])
    grad_last = fine_grad(both[:, :, 1], both[:, :, 2, :, channels:])
    grad_coarse = jnp.transpose(sums[at : at + 27 * wide].reshape(27, wide, wide), (1, 0, 2)).reshape(wide, 27 * wide)
    at += 27 * wide
    grad_up = jnp.transpose(
        sums[at : at + 8 * channels].reshape(2, 2, 2, channels, wide), (3, 0, 2, 1, 4)
    ).reshape(channels, 8 * wide)
    at += 8 * channels
    grad_down = jnp.transpose(
        sums[at : at + 4 * wide].reshape(2, 2, wide, 2, channels), (2, 0, 3, 1, 4)
    ).reshape(wide, 8 * channels)
    output = jnp.transpose(output.reshape(size_y, channels, size_x, size_z), (1, 2, 0, 3))
    return (output, grad_first, grad_down, grad_coarse, grad_up, grad_last)


def solution(mesh):
    counts = (mesh.shape["gx"], mesh.shape["gy"])
    in_specs = (P(None, "gx", "gy", None), P(), P(), P(), P(), P(), P(None, "gx", "gy", None))
    out_specs = (P(None, "gx", "gy", None), P(), P(), P(), P(), P())
    return jax.shard_map(
        functools.partial(shards, counts), mesh=mesh, in_specs=in_specs, out_specs=out_specs, check_vma=False
    )
```

```python
import functools

import jax
import jax.numpy as jnp
from jax import lax
from jax.experimental import pallas as pl
from jax.experimental.pallas import tpu as pltpu
from jax.sharding import PartitionSpec as P

MESH = pl.DeviceIdType.MESH
BF16 = jnp.bfloat16
F32 = jnp.float32
VMEM_BYTES = 56 * 1024 * 1024
LANES = 128


def leaky(values):
    return 0.505 * values + 0.495 * (jnp.sqrt(values * values + 1.0) - 1.0)


def slope_of(values):
    values = values.astype(F32)
    return 0.505 + 0.495 * values * lax.rsqrt(values * values + 1.0)


def dot(left, right):
    return jnp.dot(left, right, preferred_element_type=F32)


def dot_nt(left, right):
    return lax.dot_general(left, right, (((1,), (1,)), ((), ())), preferred_element_type=F32)


def call(kernel, args, outs, scratch, name, collective=None):
    params = dict(vmem_limit_bytes=VMEM_BYTES)
    if collective is not None:
        params.update(collective_id=collective, has_side_effects=True)
    return pl.pallas_call(
        kernel,
        out_shape=outs,
        in_specs=[pl.BlockSpec(memory_space=pltpu.VMEM)] * len(args),
        out_specs=[pl.BlockSpec(memory_space=pltpu.VMEM)] * len(outs),
        scratch_shapes=scratch,
        compiler_params=pltpu.CompilerParams(**params),
        name=name,
    )(*args)


def halo_kernel(sizes, counts, *refs):
    number = len(sizes)
    ins, outs, (send, recv) = refs[:number], refs[number : 2 * number], refs[2 * number :]
    n_x, n_y = counts
    me_x, me_y = lax.axis_index("gx"), lax.axis_index("gy")
    steps = [(i, j) for i in (-1, 0, 1) for j in (-1, 0, 1) if (i, j) != (0, 0)]

    def inside(step_x, step_y):
        at_x, at_y = me_x + step_x, me_y + step_y
        return (at_x >= 0) & (at_x < n_x) & (at_y >= 0) & (at_y < n_y)

    def place(step_x, step_y):
        return (
            jnp.clip(me_x + step_x, 0, n_x - 1),
            jnp.clip(me_y + step_y, 0, n_y - 1),
        )

    barrier = pltpu.get_barrier_semaphore()
    for step in steps:

        @pl.when(inside(*step))
        def _(step=step):
            pl.semaphore_signal(barrier, inc=1, device_id=place(*step), device_id_type=MESH)

    pl.semaphore_wait(barrier, sum(inside(*step).astype(jnp.int32) for step in steps))

    def spans(step, extent, width):
        if step == 0:
            return pl.ds(0, extent), pl.ds(width, extent)
        if step > 0:
            return pl.ds(extent - width, width), pl.ds(0, width)
        return pl.ds(0, width), pl.ds(width + extent, width)

    copies = []
    for at, (step_x, step_y) in enumerate(steps):
        for which, (row_width, lane_width) in enumerate(sizes):
            rows, lanes = ins[which].shape
            row_from, row_to = spans(step_y, rows, row_width)
            lane_from, lane_to = spans(step_x, lanes, lane_width)
            copies.append(
                (
                    step_x,
                    step_y,
                    pltpu.make_async_remote_copy(
                        src_ref=ins[which].at[row_from, lane_from],
                        dst_ref=outs[which].at[row_to, lane_to],
                        send_sem=send.at[at, which],
                        recv_sem=recv.at[at, which],
                        device_id=place(step_x, step_y),
                        device_id_type=MESH,
                    ),
                )
            )
    for step_x, step_y, copy in copies:

        @pl.when(inside(step_x, step_y))
        def _(copy=copy):
            copy.start()

    for which, (row_width, lane_width) in enumerate(sizes):
        rows, lanes = ins[which].shape
        outs[which][row_width : row_width + rows, lane_width : lane_width + lanes] = ins[which][...]
        for step_x, step_y in steps:
            row_at = {-1: (0, row_width), 0: (row_width, rows), 1: (row_width + rows, row_width)}[step_y]
            lane_at = {-1: (0, lane_width), 0: (lane_width, lanes), 1: (lane_width + lanes, lane_width)}[step_x]

            @pl.when(jnp.logical_not(inside(step_x, step_y)))
            def _(row_at=row_at, lane_at=lane_at, which=which):
                outs[which][
                    row_at[0] : row_at[0] + row_at[1], lane_at[0] : lane_at[0] + lane_at[1]
                ] = jnp.zeros((row_at[1], lane_at[1]), BF16)

    for step_x, step_y, copy in copies:

        @pl.when(inside(-step_x, -step_y))
        def _(copy=copy):
            copy.wait_recv()

    for step_x, step_y, copy in copies:

        @pl.when(inside(step_x, step_y))
        def _(copy=copy):
            copy.wait_send()


def halo(blocks, sizes, counts, collective):
    outs = [
        jax.ShapeDtypeStruct((b.shape[0] + 2 * r, b.shape[1] + 2 * l), b.dtype)
        for b, (r, l) in zip(blocks, sizes)
    ]
    scratch = [pltpu.SemaphoreType.DMA((8, len(sizes))), pltpu.SemaphoreType.DMA((8, len(sizes)))]
    return call(
        functools.partial(halo_kernel, sizes, counts),
        blocks, outs, scratch, "halo%d" % collective, collective,
    )


def sum_kernel(chunk, counts, x_ref, full, r1, s1, r2, s2, r3, send, recv):
    n_x, n_y = counts
    n_z = n_x // 2
    me_x, me_y = lax.axis_index("gx"), lax.axis_index("gy")
    core, me_z = lax.rem(me_x, 2), me_x // 2
    mid, half = chunk * n_z, chunk * n_z * n_y
    twin = (me_z * 2 + 1 - core, me_y)

    def y_peer(step):
        return lax.rem(me_y + step, n_y)

    def z_peer(step):
        return lax.rem(me_z + step, n_z)

    def y_place(step):
        return (me_x, y_peer(step))

    def z_place(step):
        return (z_peer(step) * 2 + core, me_y)

    barrier = pltpu.get_barrier_semaphore()
    peers = [twin] + [y_place(k) for k in range(1, n_y)] + [z_place(k) for k in range(1, n_z)]
    for peer in peers:
        pl.semaphore_signal(barrier, inc=1, device_id=peer, device_id_type=MESH)
    pl.semaphore_wait(barrier, len(peers))

    def copy(src, dst, at, place):
        made = pltpu.make_async_remote_copy(
            src_ref=src, dst_ref=dst, send_sem=send.at[at], recv_sem=recv.at[at],
            device_id=place, device_id_type=MESH,
        )
        made.start()
        return made

    def rows(start, size):
        return pl.ds(pl.multiple_of(start, 16), size)

    started = []
    count = 0
    mine = core * half
    one = copy(x_ref.at[rows((1 - core) * half, half)], r1, 0, twin)
    one.wait_recv()
    started.append(one)
    s1[...] = (x_ref[rows(mine, half), :].astype(F32) + r1[...].astype(F32)).astype(BF16)
    count = 1
    group = []
    for k in range(1, n_y):
        group.append(copy(s1.at[rows(y_peer(k) * mid, mid)], r2.at[k - 1], count, y_place(k)))
        count += 1
    total = s1[rows(me_y * mid, mid), :].astype(F32)
    for k, made in enumerate(group):
        made.wait_recv()
        total = total + r2[k].astype(F32)
    s2[...] = total.astype(BF16)
    started += group
    group = []
    for k in range(1, n_z):
        group.append(copy(s2.at[rows(z_peer(k) * chunk, chunk)], r3.at[k - 1], count, z_place(k)))
        count += 1
    total = s2[rows(me_z * chunk, chunk), :].astype(F32)
    for k, made in enumerate(group):
        made.wait_recv()
        total = total + r3[k].astype(F32)
    started += group
    base = mine + me_y * mid
    own = rows(base + me_z * chunk, chunk)
    full[own, :] = total.astype(BF16)
    group = []
    for k in range(1, n_z):
        group.append(copy(full.at[own], full.at[own], count, z_place(k)))
        count += 1
    for made in group:
        made.wait_recv()
    started += group
    own = rows(base, mid)
    group = []
    for k in range(1, n_y):
        group.append(copy(full.at[own], full.at[own], count, y_place(k)))
        count += 1
    for made in group:
        made.wait_recv()
    started += group
    own = rows(mine, half)
    last = copy(full.at[own], full.at[own], count, twin)
    last.wait_recv()
    started.append(last)
    for made in started:
        made.wait_send()


def sum_all(packed, chunk, counts, collective):
    n_x, n_y = counts
    n_z = n_x // 2
    copies = 2 + 2 * (n_y - 1) + 2 * (n_z - 1)
    half, mid = chunk * n_z * n_y, chunk * n_z
    scratch = [
        pltpu.VMEM((half, LANES), BF16),
        pltpu.VMEM((half, LANES), BF16),
        pltpu.VMEM((max(n_y - 1, 1), mid, LANES), BF16),
        pltpu.VMEM((mid, LANES), BF16),
        pltpu.VMEM((max(n_z - 1, 1), chunk, LANES), BF16),
        pltpu.SemaphoreType.DMA((copies,)),
        pltpu.SemaphoreType.DMA((copies,)),
    ]
    return call(
        functools.partial(sum_kernel, chunk, counts),
        [packed], [jax.ShapeDtypeStruct(packed.shape, BF16)], scratch, "sum_all", collective,
    )[0]


def parity_matrix(size, inverse):
    first = lax.broadcasted_iota(jnp.int32, (size, size), 0)
    second = lax.broadcasted_iota(jnp.int32, (size, size), 1)
    if inverse:
        first, second = second, first
    half = size // 2
    wanted = jnp.where(second < half, 2 * second, 2 * (second - half) + 1)
    return jnp.where(first == wanted, 1.0, 0.0).astype(BF16)


def moved(block, forward):
    lanes = block.shape[1]
    at = lax.broadcasted_iota(jnp.int32, block.shape, 1)
    turned = pltpu.roll(block.astype(F32), 1 if forward else lanes - 1, 1)
    return jnp.where(at == (0 if forward else lanes - 1), 0.0, turned).astype(BF16)


def fine_shifts(source, target):
    rows, lanes = source.shape
    half = LANES
    size = 2 * half
    def step(x, _):
        base = pl.multiple_of(x * size, size)
        even = source[:, pl.ds(base, half)]
        odd = source[:, pl.ds(base + half, half)]
        target[0:rows, pl.ds(base, half)] = moved(odd, True)
        target[0:rows, pl.ds(base + half, half)] = even
        target[rows : 2 * rows, pl.ds(base, half)] = even
        target[rows : 2 * rows, pl.ds(base + half, half)] = odd
        target[2 * rows : 3 * rows, pl.ds(base, half)] = odd
        target[2 * rows : 3 * rows, pl.ds(base + half, half)] = moved(even, False)
        return 0
    lax.fori_loop(0, lanes // size, step, 0)


def coarse_shifts(source, target):
    rows, lanes = source.shape
    for x in range(lanes // LANES):
        block = source[:, x * LANES : (x + 1) * LANES]
        target[0:rows, x * LANES : (x + 1) * LANES] = moved(block, True)
        target[rows : 2 * rows, x * LANES : (x + 1) * LANES] = block
        target[2 * rows : 3 * rows, x * LANES : (x + 1) * LANES] = moved(block, False)


def fine_conv(shifted, weight, store):
    size = 2 * LANES
    def step(x, _):
        total = None
        for along_x in range(3):
            base = pl.multiple_of((x + along_x) * size, size)
            term = dot(weight[along_x], shifted[:, pl.ds(base, size)])
            total = term if total is None else total + term
        store(pl.ds(pl.multiple_of(x * size, size), size), total)
        return 0
    lax.fori_loop(0, shifted.shape[1] // size - 2, step, 0)


def coarse_conv(shifted, weight):
    width = shifted.shape[1] - 2 * LANES
    total = None
    for along_x in range(3):
        term = dot(weight[along_x], shifted[:, along_x * LANES : along_x * LANES + width])
        total = term if total is None else total + term
    return total


def cells(n_qx, n_qy):
    found = []
    for a in range(2):
        for c in range(2):
            for qy in range(n_qy):
                for qx in range(n_qx):
                    found.append((2 * a + c, qy * n_qx + qx, qy, (2 * qx + a) * 2 + c))
    return found


def part(row, lane):
    return (slice(row * LANES, (row + 1) * LANES), slice(lane * LANES, (lane + 1) * LANES))


def to_wide(value, n_qy, channels):
    return jnp.concatenate([value[q * channels : (q + 1) * channels] for q in range(n_qy)], axis=1)


def left_half(shape):
    return lax.broadcasted_iota(jnp.int32, shape, 1) < shape[1] // 2


def band_fine(weight, twice, target, n_y, flipped):
    channels = weight.shape[0]
    left = left_half((channels, LANES))
    for k in range(14):
        block = weight[:, k * LANES : (k + 1) * LANES].astype(F32)
        count = min(2, 27 - 2 * k)
        if flipped:
            both = jnp.concatenate([block, block], axis=0).T
            twice[k * LANES : k * LANES + count * channels, :] = both[: count * channels]
        else:
            turned = pltpu.roll(block, channels, 1)
            twice[k * LANES : k * LANES + channels, :] = jnp.where(left, block, turned)
            if count == 2:
                twice[k * LANES + channels : (k + 1) * LANES, :] = jnp.where(left, turned, block)
    zero = jnp.zeros((channels, LANES), F32)
    width = (n_y + 2) * channels
    for along_x in range(3):
        for along_z in range(3):

            def unit(along_y):
                if along_y < 0 or along_y > 2:
                    return zero
                tap = along_x * 9 + along_y * 3 + along_z
                tap = 26 - tap if flipped else tap
                return twice[tap * channels : (tap + 1) * channels, :]

            for y in range(n_y):
                for k in range(width // LANES):
                    lane = along_z * width + k * LANES
                    target[along_x, y * channels : (y + 1) * channels, lane : lane + LANES] = jnp.where(
                        left, unit(2 * k - y), unit(2 * k + 1 - y)
                    ).astype(BF16)


def band_coarse(weight, target, n_y, flipped):
    width = (n_y + 2) * LANES
    for along_x in range(3):
        for along_z in range(3):
            for row in range(n_y + 2):
                for y in range(n_y):
                    if row - y < 0 or row - y > 2:
                        lane = along_z * width + row * LANES
                        target[along_x, y * LANES : (y + 1) * LANES, lane : lane + LANES] = jnp.zeros((LANES, LANES), BF16)
            for along_y in range(3):
                tap = along_x * 9 + along_y * 3 + along_z
                tap = 26 - tap if flipped else tap
                block = weight[:, tap * LANES : (tap + 1) * LANES]
                if flipped:
                    block = block.astype(F32).T.astype(BF16)
                for y in range(n_y):
                    lane = along_z * width + (y + along_y) * LANES
                    target[along_x, y * LANES : (y + 1) * LANES, lane : lane + LANES] = block


def down_weight(weight):
    channels = LANES // 2
    left = left_half((weight.shape[0], LANES))
    pieces = []
    for a in range(2):
        zero = weight[:, 4 * a * channels : 4 * a * channels + LANES].astype(F32)
        one = weight[:, (4 * a + 2) * channels : (4 * a + 2) * channels + LANES].astype(F32)
        pieces.append(jnp.where(left, zero, pltpu.roll(one, channels, 1)))
        pieces.append(jnp.where(left, pltpu.roll(zero, channels, 1), one))
    return jnp.concatenate(pieces, axis=1)


def up_weight(weight):
    pieces = []
    for a in range(2):
        for c in range(2):
            for b in range(2):
                tap = 4 * a + 2 * b + c
                pieces.append(weight[:, tap * LANES : (tap + 1) * LANES].astype(F32))
    return jnp.concatenate(pieces, axis=0)


def first_kernel(field, cotan, weight_first, weight_last, weight_down, hidden, coarse, back_sum, field_z, cotan_z, work, cells_ref, shifted, w_first, w_last_t, twice):
    size = 2 * LANES
    n_y = hidden.shape[0] // weight_first.shape[0]
    band_fine(weight_first, twice, w_first, n_y, False)
    band_fine(weight_last, twice, w_last_t, n_y, True)
    w_down = down_weight(weight_down).astype(BF16)
    matrix = parity_matrix(size, False)
    blocks = field.shape[1] // size
    for x in range(blocks):
        field_z[:, x * size : (x + 1) * size] = dot(field[:, x * size : (x + 1) * size], matrix).astype(BF16)
        work[:, x * size : (x + 1) * size] = dot(cotan[:, x * size : (x + 1) * size], matrix).astype(BF16)
    fine_shifts(field_z, shifted)

    def store_hidden(where, value):
        hidden[:, where] = leaky(value).astype(BF16)

    fine_conv(shifted, w_first, store_hidden)
    n_qx, n_qy = (blocks - 2) // 2, hidden.shape[0] // LANES
    for row, lane, fine_row, fine_lane in cells(n_qx, n_qy):
        cells_ref[part(row, lane)] = hidden[part(fine_row, fine_lane)]
    value = leaky(dot(w_down, cells_ref[...])).astype(BF16)
    width = n_qx * LANES
    for qy in range(n_qy):
        coarse[qy * LANES : (qy + 1) * LANES, :] = value[:, qy * width : (qy + 1) * width]
    rim = (work.shape[0] - hidden.shape[0]) // 2
    cotan_z[...] = work[rim : rim + hidden.shape[0], size : size + hidden.shape[1]]
    fine_shifts(work, shifted)

    def store_back(where, value):
        back_sum[:, where] = value

    fine_conv(shifted, w_last_t, store_back)


def level_kernel(coarse, weight_coarse, weight_up, hidden, back_sum, summed, back_level, grad_up, raised, back_cells, shifted, w_coarse):
    coarse_shifts(coarse, shifted)
    n_qx, n_qy = coarse.shape[1] // LANES - 2, coarse.shape[0] // LANES - 2
    band_coarse(weight_coarse, w_coarse, n_qy, False)
    w_up = up_weight(weight_up)
    w_up_t = w_up.T.astype(BF16)
    w_up = w_up.astype(BF16)
    level = to_wide(leaky(coarse_conv(shifted, w_coarse)).astype(BF16), n_qy, LANES)
    raised[...] = dot(w_up, level)
    for row, lane, fine_row, fine_lane in cells(n_qx, n_qy):
        here, fine = part(row, lane), part(fine_row, fine_lane)
        value = raised[here]
        root = lax.rsqrt(value * value + 1.0)
        summed[fine] = (leaky(value) + hidden[fine].astype(F32)).astype(BF16)
        back_cells[here] = (back_sum[fine] * (0.505 + 0.495 * value * root)).astype(BF16)
    grad_up[...] = dot_nt(back_cells[...], level)
    back = (dot(w_up_t, back_cells[...]) * slope_of(level)).astype(BF16)
    width = n_qx * LANES
    for qy in range(n_qy):
        back_level[qy * LANES : (qy + 1) * LANES, :] = back[:, qy * width : (qy + 1) * width]


def last_kernel(summed, back_level, coarse, hidden, back_sum, field_z, cotan_z, grad_up, weight_last, weight_coarse, weight_down, output, packed, shifted, shifted_c, back_first, cells_ref, spread, total_ref, w_last, w_coarse_t, twice):
    size = 2 * LANES
    matrix = parity_matrix(size, True)
    packed[...] = jnp.zeros(packed.shape, BF16)
    channels = 64
    n_y = hidden.shape[0] // channels
    n_qx, n_qy = coarse.shape[1] // LANES - 2, coarse.shape[0] // LANES - 2
    width = n_qx * LANES
    fine_rows = summed.shape[0]
    coarse_rows = coarse.shape[0]
    lanes = hidden.shape[1]
    in_half = left_half((channels, LANES))
    band_fine(weight_last, twice, w_last, n_y, False)
    band_coarse(weight_coarse, w_coarse_t, n_qy, True)
    w_down_t = down_weight(weight_down).T.astype(BF16)

    coarse_shifts(back_level, shifted_c)
    center = coarse[LANES : LANES * (1 + n_qy), LANES : LANES + width]
    back = (coarse_conv(shifted_c, w_coarse_t) * slope_of(center)).astype(BF16)
    back_wide = to_wide(back, n_qy, LANES)
    spread[...] = dot(w_down_t, back_wide)
    for row, lane, fine_row, fine_lane in cells(n_qx, n_qy):
        here, fine = part(row, lane), part(fine_row, fine_lane)
        mine = hidden[fine]
        cells_ref[here] = mine
        back_first[fine] = ((back_sum[fine] + spread[here]) * slope_of(mine)).astype(BF16)

    base = 27 * channels
    coarse_shifts(coarse, shifted_c)
    center = back_level[LANES : LANES * (1 + n_qy), LANES : LANES + width]
    for along_x in range(3):
        total_ref[:, : 3 * coarse_rows] = dot_nt(center, shifted_c[:, along_x * LANES : along_x * LANES + width])
        for along_z in range(3):
            for along_y in range(3):
                term = None
                for qy in range(n_qy):
                    lane = along_z * coarse_rows + (qy + along_y) * LANES
                    here = total_ref[qy * LANES : (qy + 1) * LANES, lane : lane + LANES]
                    term = here if term is None else term + here
                at = base + (along_x * 9 + along_y * 3 + along_z) * LANES
                packed[at : at + LANES, :] = term.astype(BF16)
    base = base + 27 * LANES
    for k in range(8):
        packed[base + k * 64 : base + k * 64 + 64, :] = grad_up[k * 64 : k * 64 + 64, :].astype(BF16)
    base = base + 512
    down = dot_nt(back_wide, cells_ref[...])
    for k in range(4):
        packed[base + k * LANES : base + (k + 1) * LANES, :] = down[:, k * LANES : (k + 1) * LANES].astype(BF16)

    def weight_grad(left, second):
        for along_x in range(3):
            total_ref[:, : 3 * fine_rows] = dot_nt(left[...], shifted[:, along_x * size : along_x * size + lanes])
            for along_z in range(3):
                total = None
                for y in range(n_y):
                    term = total_ref[y * channels : (y + 1) * channels, along_z * fine_rows : (along_z + 1) * fine_rows]
                    if y > 0:
                        term = pltpu.roll(term, fine_rows - channels * y, 1)
                    term = term[:, : 2 * LANES]
                    total = term if total is None else total + term
                at = (along_x * 3 + along_z) * 3 * channels
                tail = at + 2 * channels
                head = total[:, :LANES].astype(BF16)
                rest = total[:, LANES:]
                if second:
                    packed[at + channels : at + 2 * channels, :] = head
                    rest = pltpu.roll(rest, channels, 1)
                    packed[tail : tail + channels, :] = jnp.where(
                        in_half, packed[tail : tail + channels, :].astype(F32), rest
                    ).astype(BF16)
                else:
                    packed[at : at + channels, :] = head
                    packed[tail : tail + channels, :] = rest.astype(BF16)

    fine_shifts(field_z, shifted)
    weight_grad(back_first, False)
    fine_shifts(summed, shifted)
    weight_grad(cotan_z, True)

    def store(where, value):
        output[:, where] = dot(value.astype(BF16), matrix).astype(BF16)

    fine_conv(shifted, w_last, store)


def unpack_kernel(sums, first, down, coarse, up, last):
    channels = first.shape[0]
    left = left_half((channels, LANES))

    def piece(tap, which, side):
        along_x, along_y, along_z = tap // 9, tap // 3 % 3, tap % 3
        at = (along_x * 3 + along_z) * 3 * channels
        at += 2 * channels if along_y == 2 else which * channels
        held = which if along_y == 2 else along_y
        value = sums[at : at + channels, :].astype(F32)
        return value if held == side else pltpu.roll(value, channels, 1)

    for which, target in ((0, first), (1, last)):
        for k in range(13):
            target[:, k * LANES : (k + 1) * LANES] = jnp.where(
                left, piece(2 * k, which, 0), piece(2 * k + 1, which, 1)
            )
        target[:, 13 * LANES : 13 * LANES + channels] = piece(26, which, 0)[:, :channels]
    at = 27 * channels
    for k in range(27):
        coarse[:, k * LANES : (k + 1) * LANES] = sums[at + k * LANES : at + (k + 1) * LANES, :].astype(F32)
    at += 27 * LANES
    for a in range(2):
        for c in range(2):
            for b in range(2):
                tap, row = 4 * a + 2 * b + c, at + (4 * a + 2 * c + b) * channels
                up[:, tap * LANES : (tap + 1) * LANES] = sums[row : row + channels, :].astype(F32)
    at += 8 * channels
    wide_left = left_half((LANES, LANES))
    for a in range(2):
        zero = sums[at + 2 * a * LANES : at + (2 * a + 1) * LANES, :].astype(F32)
        one = sums[at + (2 * a + 1) * LANES : at + (2 * a + 2) * LANES, :].astype(F32)
        base = 2 * a * LANES
        down[:, base : base + LANES] = jnp.where(wide_left, zero, pltpu.roll(one, channels, 1))
        down[:, base + LANES : base + 2 * LANES] = jnp.where(wide_left, pltpu.roll(zero, channels, 1), one)


def shards(counts, field, weight_first, weight_down, weight_coarse, weight_up, weight_last, cotangent):
    channels, size_x, size_y, size_z = field.shape
    wide = weight_down.shape[0]
    n_qx, n_qy = size_x // 2, size_y // 2
    rows, lanes = size_y * channels, size_x * size_z
    fine = lambda v: jnp.transpose(v, (2, 0, 1, 3)).reshape(rows, lanes)
    shape = jax.ShapeDtypeStruct

    whole = lambda v: jnp.pad(v, ((0, 0), (0, channels)))
    weight_first, weight_last = whole(weight_first), whole(weight_last)
    fine_rim, coarse_rim = (channels, size_z), (wide, size_z // 2)
    field_w, cotan_w = halo([fine(field), fine(cotangent)], [fine_rim, fine_rim], counts, 0)
    full_rows, full_lanes = field_w.shape
    n_cells = n_qx * n_qy * LANES
    hidden, coarse, back_sum, field_z, cotan_z = call(
        first_kernel,
        [field_w, cotan_w, weight_first, weight_last, weight_down],
        [
            shape((rows, lanes), BF16),
            shape((n_qy * wide, n_qx * LANES), BF16),
            shape((rows, lanes), F32),
            shape((full_rows, full_lanes), BF16),
            shape((rows, lanes), BF16),
        ],
        [
            pltpu.VMEM((full_rows, full_lanes), BF16),
            pltpu.VMEM((8 * channels, n_cells), BF16),
            pltpu.VMEM((3 * full_rows, full_lanes), BF16),
            pltpu.VMEM((3, rows, 3 * full_rows), BF16),
            pltpu.VMEM((3, rows, 3 * full_rows), BF16),
            pltpu.VMEM((27 * channels, LANES), F32),
        ],
        "first",
    )
    (coarse_w,) = halo([coarse], [coarse_rim], counts, 1)
    coarse_rows, coarse_lanes = coarse_w.shape
    summed, back_level, grad_up = call(
        level_kernel,
        [coarse_w, weight_coarse, weight_up, hidden, back_sum],
        [
            shape((rows, lanes), BF16),
            shape((n_qy * wide, n_qx * LANES), BF16),
            shape((8 * channels, wide), F32),
        ],
        [
            pltpu.VMEM((8 * channels, n_cells), F32),
            pltpu.VMEM((8 * channels, n_cells), BF16),
            pltpu.VMEM((3 * coarse_rows, coarse_lanes), BF16),
            pltpu.VMEM((3, n_qy * wide, 3 * coarse_rows), BF16),
        ],
        "level",
    )
    summed_w, back_level_w = halo([summed, back_level], [fine_rim, coarse_rim], counts, 2)
    used = 27 * channels + 27 * wide + 8 * channels + 4 * wide
    devices = counts[0] * counts[1]
    chunk = -(-used // (devices * 16)) * 16
    output, packed = call(
        last_kernel,
        [summed_w, back_level_w, coarse_w, hidden, back_sum, field_z, cotan_z, grad_up, weight_last, weight_coarse, weight_down],
        [shape((rows, lanes), BF16), shape((chunk * devices, LANES), BF16)],
        [
            pltpu.VMEM((3 * full_rows, full_lanes), BF16),
            pltpu.VMEM((3 * coarse_rows, coarse_lanes), BF16),
            pltpu.VMEM((rows, lanes), BF16),
            pltpu.VMEM((8 * channels, n_cells), BF16),
            pltpu.VMEM((8 * channels, n_cells), F32),
            pltpu.VMEM((max(rows, n_qy * wide), 3 * max(full_rows, coarse_rows)), F32),
            pltpu.VMEM((3, rows, 3 * full_rows), BF16),
            pltpu.VMEM((3, n_qy * wide, 3 * coarse_rows), BF16),
            pltpu.VMEM((27 * channels, LANES), F32),
        ],
        "last",
    )
    sums = sum_all(packed, chunk, counts, 3)
    grad_first, grad_down, grad_coarse, grad_up, grad_last = call(
        unpack_kernel,
        [sums],
        [
            shape((channels, 27 * channels), F32),
            shape((wide, 8 * channels), F32),
            shape((wide, 27 * wide), F32),
            shape((channels, 8 * wide), F32),
            shape((channels, 27 * channels), F32),
        ],
        [],
        "unpack",
    )
    output = jnp.transpose(output.reshape(size_y, channels, size_x, size_z), (1, 2, 0, 3))
    return (output, grad_first, grad_down, grad_coarse, grad_up, grad_last)


def solution(mesh):
    counts = (mesh.shape["gx"], mesh.shape["gy"])
    in_specs = (P(None, "gx", "gy", None), P(), P(), P(), P(), P(), P(None, "gx", "gy", None))
    out_specs = (P(None, "gx", "gy", None), P(), P(), P(), P(), P())
    return jax.shard_map(
        functools.partial(shards, counts), mesh=mesh, in_specs=in_specs, out_specs=out_specs, check_vma=False
    )
```

```python
import functools

import jax
import jax.numpy as jnp
from jax import lax
from jax.experimental import pallas as pl
from jax.experimental.pallas import tpu as pltpu
from jax.sharding import PartitionSpec as P

MESH = pl.DeviceIdType.MESH
BF16 = jnp.bfloat16
F32 = jnp.float32
VMEM_BYTES = 56 * 1024 * 1024
LANES = 128


def leaky(values):
    return 0.505 * values + 0.495 * (jnp.sqrt(values * values + 1.0) - 1.0)


def slope_of(values):
    values = values.astype(F32)
    return 0.505 + 0.495 * values * lax.rsqrt(values * values + 1.0)


def dot(left, right):
    return jnp.dot(left, right, preferred_element_type=F32)


def dot_nt(left, right):
    return lax.dot_general(left, right, (((1,), (1,)), ((), ())), preferred_element_type=F32)


def call(kernel, args, outs, scratch, name, collective=None):
    params = dict(vmem_limit_bytes=VMEM_BYTES)
    if collective is not None:
        params.update(collective_id=collective, has_side_effects=True)
    return pl.pallas_call(
        kernel,
        out_shape=outs,
        in_specs=[pl.BlockSpec(memory_space=pltpu.VMEM)] * len(args),
        out_specs=[pl.BlockSpec(memory_space=pltpu.VMEM)] * len(outs),
        scratch_shapes=scratch,
        compiler_params=pltpu.CompilerParams(**params),
        name=name,
    )(*args)


STEPS = [(i, j) for i in (-1, 0, 1) for j in (-1, 0, 1) if (i, j) != (0, 0)]


def inside(counts, step):
    at_x, at_y = lax.axis_index("gx") + step[0], lax.axis_index("gy") + step[1]
    return (at_x >= 0) & (at_x < counts[0]) & (at_y >= 0) & (at_y < counts[1])


def place(counts, step):
    return (
        jnp.clip(lax.axis_index("gx") + step[0], 0, counts[0] - 1),
        jnp.clip(lax.axis_index("gy") + step[1], 0, counts[1] - 1),
    )


def greet(counts):
    barrier = pltpu.get_barrier_semaphore()
    for step in STEPS:

        @pl.when(inside(counts, step))
        def _(step=step):
            pl.semaphore_signal(barrier, inc=1, device_id=place(counts, step), device_id_type=MESH)

    pl.semaphore_wait(barrier, sum(inside(counts, step).astype(jnp.int32) for step in STEPS))


def clear_rim(counts, wide, rim):
    for step_x, step_y in STEPS:
        spans = []
        for step, extent, width in ((step_y, wide.shape[0], rim[0]), (step_x, wide.shape[1], rim[1])):
            start = {-1: 0, 0: width, 1: extent - width}[step]
            spans.append((start, extent - 2 * width if step == 0 else width))
        (row, rows), (lane, lanes) = spans

        @pl.when(jnp.logical_not(inside(counts, (step_x, step_y))))
        def _(row=row, rows=rows, lane=lane, lanes=lanes):
            wide[row : row + rows, lane : lane + lanes] = jnp.zeros((rows, lanes), BF16)


def send_rim(counts, wide, rim, send, recv, which):
    copies = []
    for at, step in enumerate(STEPS):
        source, target = [], []
        for move, extent, width in ((step[1], wide.shape[0], rim[0]), (step[0], wide.shape[1], rim[1])):
            if move == 0:
                source.append(pl.ds(width, extent - 2 * width))
                target.append(pl.ds(width, extent - 2 * width))
            elif move > 0:
                source.append(pl.ds(extent - 2 * width, width))
                target.append(pl.ds(0, width))
            else:
                source.append(pl.ds(width, width))
                target.append(pl.ds(extent - width, width))
        copy = pltpu.make_async_remote_copy(
            src_ref=wide.at[tuple(source)],
            dst_ref=wide.at[tuple(target)],
            send_sem=send.at[which, at],
            recv_sem=recv.at[which, at],
            device_id=place(counts, step),
            device_id_type=MESH,
        )
        copies.append((step, copy))

        @pl.when(inside(counts, step))
        def _(copy=copy):
            copy.start()

    return copies


def rim_arrived(counts, copies):
    for step, copy in copies:

        @pl.when(inside(counts, (-step[0], -step[1])))
        def _(copy=copy):
            copy.wait_recv()


def rim_left(counts, copies):
    for step, copy in copies:

        @pl.when(inside(counts, step))
        def _(copy=copy):
            copy.wait_send()


def sum_kernel(chunk, counts, x_ref, full, r1, s1, r2, s2, r3, send, recv):
    n_x, n_y = counts
    n_z = n_x // 2
    me_x, me_y = lax.axis_index("gx"), lax.axis_index("gy")
    core, me_z = lax.rem(me_x, 2), me_x // 2
    mid, half = chunk * n_z, chunk * n_z * n_y
    twin = (me_z * 2 + 1 - core, me_y)

    def y_peer(step):
        return lax.rem(me_y + step, n_y)

    def z_peer(step):
        return lax.rem(me_z + step, n_z)

    def y_place(step):
        return (me_x, y_peer(step))

    def z_place(step):
        return (z_peer(step) * 2 + core, me_y)

    barrier = pltpu.get_barrier_semaphore()
    peers = [twin] + [y_place(k) for k in range(1, n_y)] + [z_place(k) for k in range(1, n_z)]
    for peer in peers:
        pl.semaphore_signal(barrier, inc=1, device_id=peer, device_id_type=MESH)
    pl.semaphore_wait(barrier, len(peers))

    def copy(src, dst, at, place):
        made = pltpu.make_async_remote_copy(
            src_ref=src, dst_ref=dst, send_sem=send.at[at], recv_sem=recv.at[at],
            device_id=place, device_id_type=MESH,
        )
        made.start()
        return made

    def rows(start, size):
        return pl.ds(pl.multiple_of(start, 16), size)

    started = []
    count = 0
    mine = core * half
    one = copy(x_ref.at[rows((1 - core) * half, half)], r1, 0, twin)
    one.wait_recv()
    started.append(one)
    s1[...] = (x_ref[rows(mine, half), :].astype(F32) + r1[...].astype(F32)).astype(BF16)
    count = 1
    group = []
    for k in range(1, n_y):
        group.append(copy(s1.at[rows(y_peer(k) * mid, mid)], r2.at[k - 1], count, y_place(k)))
        count += 1
    total = s1[rows(me_y * mid, mid), :].astype(F32)
    for k, made in enumerate(group):
        made.wait_recv()
        total = total + r2[k].astype(F32)
    s2[...] = total.astype(BF16)
    started += group
    group = []
    for k in range(1, n_z):
        group.append(copy(s2.at[rows(z_peer(k) * chunk, chunk)], r3.at[k - 1], count, z_place(k)))
        count += 1
    total = s2[rows(me_z * chunk, chunk), :].astype(F32)
    for k, made in enumerate(group):
        made.wait_recv()
        total = total + r3[k].astype(F32)
    started += group
    base = mine + me_y * mid
    own = rows(base + me_z * chunk, chunk)
    full[own, :] = total.astype(BF16)
    group = []
    for k in range(1, n_z):
        group.append(copy(full.at[own], full.at[own], count, z_place(k)))
        count += 1
    for made in group:
        made.wait_recv()
    started += group
    own = rows(base, mid)
    group = []
    for k in range(1, n_y):
        group.append(copy(full.at[own], full.at[own], count, y_place(k)))
        count += 1
    for made in group:
        made.wait_recv()
    started += group
    own = rows(mine, half)
    last = copy(full.at[own], full.at[own], count, twin)
    last.wait_recv()
    started.append(last)
    for made in started:
        made.wait_send()


def sum_all(packed, chunk, counts, collective):
    n_x, n_y = counts
    n_z = n_x // 2
    copies = 2 + 2 * (n_y - 1) + 2 * (n_z - 1)
    half, mid = chunk * n_z * n_y, chunk * n_z
    scratch = [
        pltpu.VMEM((half, LANES), BF16),
        pltpu.VMEM((half, LANES), BF16),
        pltpu.VMEM((max(n_y - 1, 1), mid, LANES), BF16),
        pltpu.VMEM((mid, LANES), BF16),
        pltpu.VMEM((max(n_z - 1, 1), chunk, LANES), BF16),
        pltpu.SemaphoreType.DMA((copies,)),
        pltpu.SemaphoreType.DMA((copies,)),
    ]
    return call(
        functools.partial(sum_kernel, chunk, counts),
        [packed], [jax.ShapeDtypeStruct(packed.shape, BF16)], scratch, "sum_all", collective,
    )[0]


def parity_matrix(size, inverse):
    first = lax.broadcasted_iota(jnp.int32, (size, size), 0)
    second = lax.broadcasted_iota(jnp.int32, (size, size), 1)
    if inverse:
        first, second = second, first
    half = size // 2
    wanted = jnp.where(second < half, 2 * second, 2 * (second - half) + 1)
    return jnp.where(first == wanted, 1.0, 0.0).astype(BF16)


def moved(block, forward):
    lanes = block.shape[1]
    at = lax.broadcasted_iota(jnp.int32, block.shape, 1)
    turned = pltpu.roll(block.astype(F32), 1 if forward else lanes - 1, 1)
    return jnp.where(at == (0 if forward else lanes - 1), 0.0, turned).astype(BF16)


def fine_shifts(source, target):
    rows, lanes = source.shape
    half = LANES
    size = 2 * half
    def step(x, _):
        base = pl.multiple_of(x * size, size)
        even = source[:, pl.ds(base, half)]
        odd = source[:, pl.ds(base + half, half)]
        target[0:rows, pl.ds(base, half)] = moved(odd, True)
        target[0:rows, pl.ds(base + half, half)] = even
        target[rows : 2 * rows, pl.ds(base, half)] = even
        target[rows : 2 * rows, pl.ds(base + half, half)] = odd
        target[2 * rows : 3 * rows, pl.ds(base, half)] = odd
        target[2 * rows : 3 * rows, pl.ds(base + half, half)] = moved(even, False)
        return 0
    lax.fori_loop(0, lanes // size, step, 0)


def coarse_shifts(source, target):
    rows, lanes = source.shape
    for x in range(lanes // LANES):
        block = source[:, x * LANES : (x + 1) * LANES]
        target[0:rows, x * LANES : (x + 1) * LANES] = moved(block, True)
        target[rows : 2 * rows, x * LANES : (x + 1) * LANES] = block
        target[2 * rows : 3 * rows, x * LANES : (x + 1) * LANES] = moved(block, False)


def fine_conv(shifted, weight, store):
    size = 2 * LANES
    def step(x, _):
        total = None
        for along_x in range(3):
            base = pl.multiple_of((x + along_x) * size, size)
            term = dot(weight[along_x], shifted[:, pl.ds(base, size)])
            total = term if total is None else total + term
        store(pl.ds(pl.multiple_of(x * size, size), size), total)
        return 0
    lax.fori_loop(0, shifted.shape[1] // size - 2, step, 0)


def coarse_conv(shifted, weight):
    width = shifted.shape[1] - 2 * LANES
    total = None
    for along_x in range(3):
        term = dot(weight[along_x], shifted[:, along_x * LANES : along_x * LANES + width])
        total = term if total is None else total + term
    return total


def cells(n_qx, n_qy):
    found = []
    for a in range(2):
        for c in range(2):
            for qy in range(n_qy):
                for qx in range(n_qx):
                    found.append((2 * a + c, qy * n_qx + qx, qy, (2 * qx + a) * 2 + c))
    return found


def part(row, lane):
    return (slice(row * LANES, (row + 1) * LANES), slice(lane * LANES, (lane + 1) * LANES))


def to_wide(value, n_qy, channels):
    return jnp.concatenate([value[q * channels : (q + 1) * channels] for q in range(n_qy)], axis=1)


def left_half(shape):
    return lax.broadcasted_iota(jnp.int32, shape, 1) < shape[1] // 2


def band_fine(weight, twice, target, n_y, flipped):
    channels = weight.shape[0]
    left = left_half((channels, LANES))
    for k in range(14):
        block = weight[:, k * LANES : (k + 1) * LANES].astype(F32)
        count = min(2, 27 - 2 * k)
        if flipped:
            both = jnp.concatenate([block, block], axis=0).T
            twice[k * LANES : k * LANES + count * channels, :] = both[: count * channels]
        else:
            turned = pltpu.roll(block, channels, 1)
            twice[k * LANES : k * LANES + channels, :] = jnp.where(left, block, turned)
            if count == 2:
                twice[k * LANES + channels : (k + 1) * LANES, :] = jnp.where(left, turned, block)
    zero = jnp.zeros((channels, LANES), F32)
    width = (n_y + 2) * channels
    for along_x in range(3):
        for along_z in range(3):

            def unit(along_y):
                if along_y < 0 or along_y > 2:
                    return zero
                tap = along_x * 9 + along_y * 3 + along_z
                tap = 26 - tap if flipped else tap
                return twice[tap * channels : (tap + 1) * channels, :]

            for y in range(n_y):
                for k in range(width // LANES):
                    lane = along_z * width + k * LANES
                    target[along_x, y * channels : (y + 1) * channels, lane : lane + LANES] = jnp.where(
                        left, unit(2 * k - y), unit(2 * k + 1 - y)
                    ).astype(BF16)


def band_coarse(weight, target, n_y, flipped):
    width = (n_y + 2) * LANES
    for along_x in range(3):
        for along_z in range(3):
            for row in range(n_y + 2):
                for y in range(n_y):
                    if row - y < 0 or row - y > 2:
                        lane = along_z * width + row * LANES
                        target[along_x, y * LANES : (y + 1) * LANES, lane : lane + LANES] = jnp.zeros((LANES, LANES), BF16)
            for along_y in range(3):
                tap = along_x * 9 + along_y * 3 + along_z
                tap = 26 - tap if flipped else tap
                block = weight[:, tap * LANES : (tap + 1) * LANES]
                if flipped:
                    block = block.astype(F32).T.astype(BF16)
                for y in range(n_y):
                    lane = along_z * width + (y + along_y) * LANES
                    target[along_x, y * LANES : (y + 1) * LANES, lane : lane + LANES] = block


def down_weight(weight):
    channels = LANES // 2
    left = left_half((weight.shape[0], LANES))
    pieces = []
    for a in range(2):
        zero = weight[:, 4 * a * channels : 4 * a * channels + LANES].astype(F32)
        one = weight[:, (4 * a + 2) * channels : (4 * a + 2) * channels + LANES].astype(F32)
        pieces.append(jnp.where(left, zero, pltpu.roll(one, channels, 1)))
        pieces.append(jnp.where(left, pltpu.roll(zero, channels, 1), one))
    return jnp.concatenate(pieces, axis=1)


def up_weight(weight):
    pieces = []
    for a in range(2):
        for c in range(2):
            for b in range(2):
                tap = 4 * a + 2 * b + c
                pieces.append(weight[:, tap * LANES : (tap + 1) * LANES].astype(F32))
    return jnp.concatenate(pieces, axis=0)


def block_kernel(
    counts, field, cotan, weight_first, weight_last, weight_down, weight_coarse, weight_up,
    output, packed,
    field_w, cotan_w, summed_w, coarse_w, level_w, hidden, back_sum, back_first,
    shifted, shifted_c, w_first, w_last_t, w_last, w_coarse, w_coarse_t, twice,
    cells_ref, cells_f32, total_ref, send, recv,
):
    size = 2 * LANES
    channels = weight_first.shape[0]
    rows, lanes = field.shape
    n_x, n_y = lanes // size, rows // channels
    n_qx, n_qy = n_x // 2, n_y // 2
    width = n_qx * LANES
    fine_rows, coarse_rows = field_w.shape[0], coarse_w.shape[0]
    fine_rim, coarse_rim = (channels, size), (LANES, LANES)
    left = left_half((channels, LANES))
    n_cells = n_qx * n_qy * LANES

    for wide in (field_w, cotan_w, summed_w):
        clear_rim(counts, wide, fine_rim)
    for wide in (coarse_w, level_w):
        clear_rim(counts, wide, coarse_rim)
    matrix = parity_matrix(size, False)
    for source, wide in ((field, field_w), (cotan, cotan_w)):
        for x in range(n_x):
            wide[channels : channels + rows, (x + 1) * size : (x + 2) * size] = dot(
                source[:, x * size : (x + 1) * size], matrix
            ).astype(BF16)
    greet(counts)
    copies = [send_rim(counts, field_w, fine_rim, send, recv, 0)]
    copies.append(send_rim(counts, cotan_w, fine_rim, send, recv, 1))

    band_fine(weight_first, twice, w_first, n_y, False)
    band_fine(weight_last, twice, w_last_t, n_y, True)
    band_coarse(weight_coarse, w_coarse, n_qy, False)
    w_down = down_weight(weight_down)
    w_down_t = w_down.T.astype(BF16)
    w_down = w_down.astype(BF16)
    w_up = up_weight(weight_up)
    w_up_t = w_up.T.astype(BF16)
    w_up = w_up.astype(BF16)

    rim_arrived(counts, copies[0])
    fine_shifts(field_w, shifted)

    def store_hidden(where, value):
        hidden[:, where] = leaky(value).astype(BF16)

    fine_conv(shifted, w_first, store_hidden)
    for row, lane, fine_row, fine_lane in cells(n_qx, n_qy):
        cells_ref[part(row, lane)] = hidden[part(fine_row, fine_lane)]
    value = leaky(dot(w_down, cells_ref[...])).astype(BF16)
    for qy in range(n_qy):
        coarse_w[(qy + 1) * LANES : (qy + 2) * LANES, LANES : LANES + width] = value[:, qy * width : (qy + 1) * width]
    copies.append(send_rim(counts, coarse_w, coarse_rim, send, recv, 2))

    rim_arrived(counts, copies[1])
    fine_shifts(cotan_w, shifted)

    def store_back(where, value):
        back_sum[:, where] = value

    fine_conv(shifted, w_last_t, store_back)

    rim_arrived(counts, copies[2])
    coarse_shifts(coarse_w, shifted_c)
    level = to_wide(leaky(coarse_conv(shifted_c, w_coarse)).astype(BF16), n_qy, LANES)
    cells_f32[...] = dot(w_up, level)
    for row, lane, fine_row, fine_lane in cells(n_qx, n_qy):
        here, fine = part(row, lane), part(fine_row, fine_lane)
        value = cells_f32[here]
        root = lax.rsqrt(value * value + 1.0)
        summed_w[
            channels + fine_row * LANES : channels + (fine_row + 1) * LANES,
            size + fine_lane * LANES : size + (fine_lane + 1) * LANES,
        ] = (leaky(value) + hidden[fine].astype(F32)).astype(BF16)
        cells_ref[here] = (back_sum[fine] * (0.505 + 0.495 * value * root)).astype(BF16)
    back = (dot(w_up_t, cells_ref[...]) * slope_of(level)).astype(BF16)
    for qy in range(n_qy):
        level_w[(qy + 1) * LANES : (qy + 2) * LANES, LANES : LANES + width] = back[:, qy * width : (qy + 1) * width]
    copies.append(send_rim(counts, level_w, coarse_rim, send, recv, 3))
    copies.append(send_rim(counts, summed_w, fine_rim, send, recv, 4))

    packed[...] = jnp.zeros(packed.shape, BF16)
    base = 27 * channels + 27 * LANES
    packed[base : base + 8 * channels, :] = dot_nt(cells_ref[...], level).astype(BF16)
    base = 27 * channels
    center = level_w[LANES : LANES * (1 + n_qy), LANES : LANES + width]
    for along_x in range(3):
        total_ref[:, : 3 * coarse_rows] = dot_nt(center, shifted_c[:, along_x * LANES : along_x * LANES + width])
        for along_z in range(3):
            for along_y in range(3):
                term = None
                for qy in range(n_qy):
                    lane = along_z * coarse_rows + (qy + along_y) * LANES
                    here = total_ref[qy * LANES : (qy + 1) * LANES, lane : lane + LANES]
                    term = here if term is None else term + here
                at = base + (along_x * 9 + along_y * 3 + along_z) * LANES
                packed[at : at + LANES, :] = term.astype(BF16)
    band_coarse(weight_coarse, w_coarse_t, n_qy, True)
    band_fine(weight_last, twice, w_last, n_y, False)
    fine_shifts(field_w, shifted)

    rim_arrived(counts, copies[3])
    coarse_shifts(level_w, shifted_c)
    center = coarse_w[LANES : LANES * (1 + n_qy), LANES : LANES + width]
    back = to_wide((coarse_conv(shifted_c, w_coarse_t) * slope_of(center)).astype(BF16), n_qy, LANES)
    cells_f32[...] = dot(w_down_t, back)
    for row, lane, fine_row, fine_lane in cells(n_qx, n_qy):
        here, fine = part(row, lane), part(fine_row, fine_lane)
        mine = hidden[fine]
        cells_ref[here] = mine
        back_first[fine] = ((back_sum[fine] + cells_f32[here]) * slope_of(mine)).astype(BF16)
    base = 27 * channels + 27 * LANES + 8 * channels
    down = dot_nt(back, cells_ref[...])
    for k in range(4):
        packed[base + k * LANES : base + (k + 1) * LANES, :] = down[:, k * LANES : (k + 1) * LANES].astype(BF16)

    def weight_grad(value, second):
        for along_x in range(3):
            total_ref[:, : 3 * fine_rows] = dot_nt(value, shifted[:, along_x * size : along_x * size + lanes])
            for along_z in range(3):
                total = None
                for y in range(n_y):
                    term = total_ref[y * channels : (y + 1) * channels, along_z * fine_rows : (along_z + 1) * fine_rows]
                    if y > 0:
                        term = pltpu.roll(term, fine_rows - channels * y, 1)
                    term = term[:, : 2 * LANES]
                    total = term if total is None else total + term
                at = (along_x * 3 + along_z) * 3 * channels
                tail = at + 2 * channels
                head = total[:, :LANES].astype(BF16)
                rest = total[:, LANES:]
                if second:
                    packed[at + channels : at + 2 * channels, :] = head
                    rest = pltpu.roll(rest, channels, 1)
                    packed[tail : tail + channels, :] = jnp.where(
                        left, packed[tail : tail + channels, :].astype(F32), rest
                    ).astype(BF16)
                else:
                    packed[at : at + channels, :] = head
                    packed[tail : tail + channels, :] = rest.astype(BF16)

    weight_grad(back_first[...], False)
    rim_arrived(counts, copies[4])
    fine_shifts(summed_w, shifted)
    weight_grad(cotan_w[channels : channels + rows, size : size + lanes], True)
    matrix = parity_matrix(size, True)

    def store(where, value):
        output[:, where] = dot(value.astype(BF16), matrix).astype(BF16)

    fine_conv(shifted, w_last, store)
    for group in copies:
        rim_left(counts, group)


def unpack_kernel(sums, first, down, coarse, up, last):
    channels = first.shape[0]
    left = left_half((channels, LANES))

    def piece(tap, which, side):
        along_x, along_y, along_z = tap // 9, tap // 3 % 3, tap % 3
        at = (along_x * 3 + along_z) * 3 * channels
        at += 2 * channels if along_y == 2 else which * channels
        held = which if along_y == 2 else along_y
        value = sums[at : at + channels, :].astype(F32)
        return value if held == side else pltpu.roll(value, channels, 1)

    for which, target in ((0, first), (1, last)):
        for k in range(13):
            target[:, k * LANES : (k + 1) * LANES] = jnp.where(
                left, piece(2 * k, which, 0), piece(2 * k + 1, which, 1)
            )
        target[:, 13 * LANES : 13 * LANES + channels] = piece(26, which, 0)[:, :channels]
    at = 27 * channels
    for k in range(27):
        coarse[:, k * LANES : (k + 1) * LANES] = sums[at + k * LANES : at + (k + 1) * LANES, :].astype(F32)
    at += 27 * LANES
    for a in range(2):
        for c in range(2):
            for b in range(2):
                tap, row = 4 * a + 2 * b + c, at + (4 * a + 2 * c + b) * channels
                up[:, tap * LANES : (tap + 1) * LANES] = sums[row : row + channels, :].astype(F32)
    at += 8 * channels
    wide_left = left_half((LANES, LANES))
    for a in range(2):
        zero = sums[at + 2 * a * LANES : at + (2 * a + 1) * LANES, :].astype(F32)
        one = sums[at + (2 * a + 1) * LANES : at + (2 * a + 2) * LANES, :].astype(F32)
        base = 2 * a * LANES
        down[:, base : base + LANES] = jnp.where(wide_left, zero, pltpu.roll(one, channels, 1))
        down[:, base + LANES : base + 2 * LANES] = jnp.where(wide_left, pltpu.roll(zero, channels, 1), one)


def shards(counts, field, weight_first, weight_down, weight_coarse, weight_up, weight_last, cotangent):
    channels, size_x, size_y, size_z = field.shape
    wide = weight_down.shape[0]
    n_qx, n_qy = size_x // 2, size_y // 2
    rows, lanes = size_y * channels, size_x * size_z
    fine = lambda v: jnp.transpose(v, (2, 0, 1, 3)).reshape(rows, lanes)
    shape = jax.ShapeDtypeStruct

    whole = lambda v: jnp.pad(v, ((0, 0), (0, channels)))
    weight_first, weight_last = whole(weight_first), whole(weight_last)
    wide_rows, wide_lanes = (size_y + 2) * channels, (size_x + 2) * size_z
    coarse_rows, coarse_lanes = (n_qy + 2) * wide, (n_qx + 2) * LANES
    n_cells = n_qx * n_qy * LANES
    used = 27 * channels + 27 * wide + 8 * channels + 4 * wide
    devices = counts[0] * counts[1]
    chunk = -(-used // (devices * 16)) * 16
    output, packed = call(
        functools.partial(block_kernel, counts),
        [fine(field), fine(cotangent), weight_first, weight_last, weight_down, weight_coarse, weight_up],
        [shape((rows, lanes), BF16), shape((chunk * devices, LANES), BF16)],
        [pltpu.VMEM((wide_rows, wide_lanes), BF16)] * 3
        + [pltpu.VMEM((coarse_rows, coarse_lanes), BF16)] * 2
        + [
            pltpu.VMEM((rows, lanes), BF16),
            pltpu.VMEM((rows, lanes), F32),
            pltpu.VMEM((rows, lanes), BF16),
            pltpu.VMEM((3 * wide_rows, wide_lanes), BF16),
            pltpu.VMEM((3 * coarse_rows, coarse_lanes), BF16),
        ]
        + [pltpu.VMEM((3, rows, 3 * wide_rows), BF16)] * 3
        + [pltpu.VMEM((3, n_qy * wide, 3 * coarse_rows), BF16)] * 2
        + [
            pltpu.VMEM((27 * channels, LANES), F32),
            pltpu.VMEM((8 * channels, n_cells), BF16),
            pltpu.VMEM((8 * channels, n_cells), F32),
            pltpu.VMEM((max(rows, n_qy * wide), 3 * max(wide_rows, coarse_rows)), F32),
            pltpu.SemaphoreType.DMA((5, 8)),
            pltpu.SemaphoreType.DMA((5, 8)),
        ],
        "block",
        0,
    )
    sums = sum_all(packed, chunk, counts, 3)
    grad_first, grad_down, grad_coarse, grad_up, grad_last = call(
        unpack_kernel,
        [sums],
        [
            shape((channels, 27 * channels), F32),
            shape((wide, 8 * channels), F32),
            shape((wide, 27 * wide), F32),
            shape((channels, 8 * wide), F32),
            shape((channels, 27 * channels), F32),
        ],
        [],
        "unpack",
    )
    output = jnp.transpose(output.reshape(size_y, channels, size_x, size_z), (1, 2, 0, 3))
    return (output, grad_first, grad_down, grad_coarse, grad_up, grad_last)


def solution(mesh):
    counts = (mesh.shape["gx"], mesh.shape["gy"])
    in_specs = (P(None, "gx", "gy", None), P(), P(), P(), P(), P(), P(None, "gx", "gy", None))
    out_specs = (P(None, "gx", "gy", None), P(), P(), P(), P(), P())
    return jax.shard_map(
        functools.partial(shards, counts), mesh=mesh, in_specs=in_specs, out_specs=out_specs, check_vma=False
    )
```

```python
import functools

import jax
import jax.numpy as jnp
from jax import lax
from jax.experimental import pallas as pl
from jax.experimental.pallas import tpu as pltpu
from jax.sharding import PartitionSpec as P

MESH = pl.DeviceIdType.MESH
BF16 = jnp.bfloat16
F32 = jnp.float32
VMEM_BYTES = 56 * 1024 * 1024
LANES = 128


def leaky(values):
    return 0.505 * values + 0.495 * (jnp.sqrt(values * values + 1.0) - 1.0)


def slope_of(values):
    values = values.astype(F32)
    return 0.505 + 0.495 * values * lax.rsqrt(values * values + 1.0)


def dot(left, right):
    return jnp.dot(left, right, preferred_element_type=F32)


def dot_nt(left, right):
    return lax.dot_general(left, right, (((1,), (1,)), ((), ())), preferred_element_type=F32)


def call(kernel, args, outs, scratch, name, collective=None):
    params = dict(vmem_limit_bytes=VMEM_BYTES)
    if collective is not None:
        params.update(collective_id=collective, has_side_effects=True)
    return pl.pallas_call(
        kernel,
        out_shape=outs,
        in_specs=[pl.BlockSpec(memory_space=pltpu.VMEM)] * len(args),
        out_specs=[pl.BlockSpec(memory_space=pltpu.VMEM)] * len(outs),
        scratch_shapes=scratch,
        compiler_params=pltpu.CompilerParams(**params),
        name=name,
    )(*args)


STEPS = [(i, j) for i in (-1, 0, 1) for j in (-1, 0, 1) if (i, j) != (0, 0)]


def inside(counts, step):
    at_x, at_y = lax.axis_index("gx") + step[0], lax.axis_index("gy") + step[1]
    return (at_x >= 0) & (at_x < counts[0]) & (at_y >= 0) & (at_y < counts[1])


def place(counts, step):
    return (
        jnp.clip(lax.axis_index("gx") + step[0], 0, counts[0] - 1),
        jnp.clip(lax.axis_index("gy") + step[1], 0, counts[1] - 1),
    )


def greet(counts):
    barrier = pltpu.get_barrier_semaphore()
    for step in STEPS:

        @pl.when(inside(counts, step))
        def _(step=step):
            pl.semaphore_signal(barrier, inc=1, device_id=place(counts, step), device_id_type=MESH)

    pl.semaphore_wait(barrier, sum(inside(counts, step).astype(jnp.int32) for step in STEPS))


def clear_rim(counts, wide, rim):
    for step_x, step_y in STEPS:
        spans = []
        for step, extent, width in ((step_y, wide.shape[0], rim[0]), (step_x, wide.shape[1], rim[1])):
            start = {-1: 0, 0: width, 1: extent - width}[step]
            spans.append((start, extent - 2 * width if step == 0 else width))
        (row, rows), (lane, lanes) = spans

        @pl.when(jnp.logical_not(inside(counts, (step_x, step_y))))
        def _(row=row, rows=rows, lane=lane, lanes=lanes):
            wide[row : row + rows, lane : lane + lanes] = jnp.zeros((rows, lanes), BF16)


def send_rim(counts, wide, rim, send, recv, which):
    copies = []
    for at, step in enumerate(STEPS):
        source, target = [], []
        for move, extent, width in ((step[1], wide.shape[0], rim[0]), (step[0], wide.shape[1], rim[1])):
            if move == 0:
                source.append(pl.ds(width, extent - 2 * width))
                target.append(pl.ds(width, extent - 2 * width))
            elif move > 0:
                source.append(pl.ds(extent - 2 * width, width))
                target.append(pl.ds(0, width))
            else:
                source.append(pl.ds(width, width))
                target.append(pl.ds(extent - width, width))
        copy = pltpu.make_async_remote_copy(
            src_ref=wide.at[tuple(source)],
            dst_ref=wide.at[tuple(target)],
            send_sem=send.at[which, at],
            recv_sem=recv.at[which, at],
            device_id=place(counts, step),
            device_id_type=MESH,
        )
        copies.append((step, copy))

        @pl.when(inside(counts, step))
        def _(copy=copy):
            copy.start()

    return copies


def rim_arrived(counts, copies):
    for step, copy in copies:

        @pl.when(inside(counts, (-step[0], -step[1])))
        def _(copy=copy):
            copy.wait_recv()


def rim_left(counts, copies):
    for step, copy in copies:

        @pl.when(inside(counts, step))
        def _(copy=copy):
            copy.wait_send()


def sum_kernel(chunks, counts, x_ref, full, *refs):
    send, recv = refs[-2:]
    streams, start = [], 0
    greet_sum(counts)
    for k, chunk in enumerate(chunks):
        size = chunk * counts[0] * counts[1]
        part_of = pl.ds(start, size)
        streams.append(
            sum_stream(
                chunk, counts, x_ref.at[part_of], full.at[part_of],
                *refs[5 * k : 5 * k + 5], send.at[k], recv.at[k],
            )
        )
        start += size
    ended = object()
    while streams:
        streams = [stream for stream in streams if next(stream, ended) is not ended]


def greet_sum(counts):
    n_x, n_y = counts
    n_z = n_x // 2
    me_x, me_y = lax.axis_index("gx"), lax.axis_index("gy")
    core, me_z = lax.rem(me_x, 2), me_x // 2
    peers = [(me_z * 2 + 1 - core, me_y)]
    peers += [(me_x, lax.rem(me_y + k, n_y)) for k in range(1, n_y)]
    peers += [(lax.rem(me_z + k, n_z) * 2 + core, me_y) for k in range(1, n_z)]
    barrier = pltpu.get_barrier_semaphore()
    for peer in peers:
        pl.semaphore_signal(barrier, inc=1, device_id=peer, device_id_type=MESH)
    pl.semaphore_wait(barrier, len(peers))


def sum_stream(chunk, counts, x_ref, full, r1, s1, r2, s2, r3, send, recv):
    n_x, n_y = counts
    n_z = n_x // 2
    me_x, me_y = lax.axis_index("gx"), lax.axis_index("gy")
    core, me_z = lax.rem(me_x, 2), me_x // 2
    mid, half = chunk * n_z, chunk * n_z * n_y
    twin = (me_z * 2 + 1 - core, me_y)

    def y_peer(step):
        return lax.rem(me_y + step, n_y)

    def z_peer(step):
        return lax.rem(me_z + step, n_z)

    def y_place(step):
        return (me_x, y_peer(step))

    def z_place(step):
        return (z_peer(step) * 2 + core, me_y)

    def copy(src, dst, at, place):
        made = pltpu.make_async_remote_copy(
            src_ref=src, dst_ref=dst, send_sem=send.at[at], recv_sem=recv.at[at],
            device_id=place, device_id_type=MESH,
        )
        made.start()
        return made

    def rows(start, size):
        return pl.ds(pl.multiple_of(start, 16), size)

    started = []
    count = 0
    mine = core * half
    one = copy(x_ref.at[rows((1 - core) * half, half)], r1, 0, twin)
    yield
    one.wait_recv()
    started.append(one)
    s1[...] = (x_ref[rows(mine, half), :].astype(F32) + r1[...].astype(F32)).astype(BF16)
    count = 1
    group = []
    for k in range(1, n_y):
        group.append(copy(s1.at[rows(y_peer(k) * mid, mid)], r2.at[k - 1], count, y_place(k)))
        count += 1
    yield
    total = s1[rows(me_y * mid, mid), :].astype(F32)
    for k, made in enumerate(group):
        made.wait_recv()
        total = total + r2[k].astype(F32)
    s2[...] = total.astype(BF16)
    started += group
    group = []
    for k in range(1, n_z):
        group.append(copy(s2.at[rows(z_peer(k) * chunk, chunk)], r3.at[k - 1], count, z_place(k)))
        count += 1
    yield
    total = s2[rows(me_z * chunk, chunk), :].astype(F32)
    for k, made in enumerate(group):
        made.wait_recv()
        total = total + r3[k].astype(F32)
    started += group
    base = mine + me_y * mid
    own = rows(base + me_z * chunk, chunk)
    full[own, :] = total.astype(BF16)
    group = []
    for k in range(1, n_z):
        group.append(copy(full.at[own], full.at[own], count, z_place(k)))
        count += 1
    yield
    for made in group:
        made.wait_recv()
    started += group
    own = rows(base, mid)
    group = []
    for k in range(1, n_y):
        group.append(copy(full.at[own], full.at[own], count, y_place(k)))
        count += 1
    yield
    for made in group:
        made.wait_recv()
    started += group
    own = rows(mine, half)
    last = copy(full.at[own], full.at[own], count, twin)
    yield
    last.wait_recv()
    started.append(last)
    for made in started:
        made.wait_send()


def sum_all(packed, chunks, counts, collective):
    n_x, n_y = counts
    n_z = n_x // 2
    copies = 2 + 2 * (n_y - 1) + 2 * (n_z - 1)
    scratch = []
    for chunk in chunks:
        half, mid = chunk * n_z * n_y, chunk * n_z
        scratch += [
            pltpu.VMEM((half, LANES), BF16),
            pltpu.VMEM((half, LANES), BF16),
            pltpu.VMEM((max(n_y - 1, 1), mid, LANES), BF16),
            pltpu.VMEM((mid, LANES), BF16),
            pltpu.VMEM((max(n_z - 1, 1), chunk, LANES), BF16),
        ]
    scratch += [pltpu.SemaphoreType.DMA((len(chunks), copies))] * 2
    return call(
        functools.partial(sum_kernel, chunks, counts),
        [packed], [jax.ShapeDtypeStruct(packed.shape, BF16)], scratch, "sum_all", collective,
    )[0]


def parity_matrix(size, inverse):
    first = lax.broadcasted_iota(jnp.int32, (size, size), 0)
    second = lax.broadcasted_iota(jnp.int32, (size, size), 1)
    if inverse:
        first, second = second, first
    half = size // 2
    wanted = jnp.where(second < half, 2 * second, 2 * (second - half) + 1)
    return jnp.where(first == wanted, 1.0, 0.0).astype(BF16)


def moved(block, forward):
    lanes = block.shape[1]
    at = lax.broadcasted_iota(jnp.int32, block.shape, 1)
    turned = pltpu.roll(block.astype(F32), 1 if forward else lanes - 1, 1)
    return jnp.where(at == (0 if forward else lanes - 1), 0.0, turned).astype(BF16)


def fine_shifts(source, target):
    rows, lanes = source.shape
    half = LANES
    size = 2 * half
    def step(x, _):
        base = pl.multiple_of(x * size, size)
        even = source[:, pl.ds(base, half)]
        odd = source[:, pl.ds(base + half, half)]
        target[0:rows, pl.ds(base, half)] = moved(odd, True)
        target[0:rows, pl.ds(base + half, half)] = even
        target[rows : 2 * rows, pl.ds(base, half)] = even
        target[rows : 2 * rows, pl.ds(base + half, half)] = odd
        target[2 * rows : 3 * rows, pl.ds(base, half)] = odd
        target[2 * rows : 3 * rows, pl.ds(base + half, half)] = moved(even, False)
        return 0
    lax.fori_loop(0, lanes // size, step, 0)


def coarse_shifts(source, target):
    rows, lanes = source.shape
    for x in range(lanes // LANES):
        block = source[:, x * LANES : (x + 1) * LANES]
        target[0:rows, x * LANES : (x + 1) * LANES] = moved(block, True)
        target[rows : 2 * rows, x * LANES : (x + 1) * LANES] = block
        target[2 * rows : 3 * rows, x * LANES : (x + 1) * LANES] = moved(block, False)


def fine_conv(shifted, weight, store):
    size = 2 * LANES
    def step(x, _):
        total = None
        for along_x in range(3):
            base = pl.multiple_of((x + along_x) * size, size)
            term = dot(weight[along_x], shifted[:, pl.ds(base, size)])
            total = term if total is None else total + term
        store(pl.ds(pl.multiple_of(x * size, size), size), total)
        return 0
    lax.fori_loop(0, shifted.shape[1] // size - 2, step, 0)


def coarse_conv(shifted, weight):
    width = shifted.shape[1] - 2 * LANES
    total = None
    for along_x in range(3):
        term = dot(weight[along_x], shifted[:, along_x * LANES : along_x * LANES + width])
        total = term if total is None else total + term
    return total


def cells(n_qx, n_qy):
    found = []
    for a in range(2):
        for c in range(2):
            for qy in range(n_qy):
                for qx in range(n_qx):
                    found.append((2 * a + c, qy * n_qx + qx, qy, (2 * qx + a) * 2 + c))
    return found


def part(row, lane):
    return (slice(row * LANES, (row + 1) * LANES), slice(lane * LANES, (lane + 1) * LANES))


def to_wide(value, n_qy, channels):
    return jnp.concatenate([value[q * channels : (q + 1) * channels] for q in range(n_qy)], axis=1)


def left_half(shape):
    return lax.broadcasted_iota(jnp.int32, shape, 1) < shape[1] // 2


def band_fine(weight, twice, target, n_y, flipped):
    channels = weight.shape[0]
    left = left_half((channels, LANES))
    for k in range(14):
        block = weight[:, k * LANES : (k + 1) * LANES].astype(F32)
        count = min(2, 27 - 2 * k)
        if flipped:
            both = jnp.concatenate([block, block], axis=0).T
            twice[k * LANES : k * LANES + count * channels, :] = both[: count * channels]
        else:
            turned = pltpu.roll(block, channels, 1)
            twice[k * LANES : k * LANES + channels, :] = jnp.where(left, block, turned)
            if count == 2:
                twice[k * LANES + channels : (k + 1) * LANES, :] = jnp.where(left, turned, block)
    zero = jnp.zeros((channels, LANES), F32)
    width = (n_y + 2) * channels
    for along_x in range(3):
        for along_z in range(3):

            def unit(along_y):
                if along_y < 0 or along_y > 2:
                    return zero
                tap = along_x * 9 + along_y * 3 + along_z
                tap = 26 - tap if flipped else tap
                return twice[tap * channels : (tap + 1) * channels, :]

            for y in range(n_y):
                for k in range(width // LANES):
                    lane = along_z * width + k * LANES
                    target[along_x, y * channels : (y + 1) * channels, lane : lane + LANES] = jnp.where(
                        left, unit(2 * k - y), unit(2 * k + 1 - y)
                    ).astype(BF16)


def band_coarse(weight, target, n_y, flipped):
    width = (n_y + 2) * LANES
    for along_x in range(3):
        for along_z in range(3):
            for row in range(n_y + 2):
                for y in range(n_y):
                    if row - y < 0 or row - y > 2:
                        lane = along_z * width + row * LANES
                        target[along_x, y * LANES : (y + 1) * LANES, lane : lane + LANES] = jnp.zeros((LANES, LANES), BF16)
            for along_y in range(3):
                tap = along_x * 9 + along_y * 3 + along_z
                tap = 26 - tap if flipped else tap
                block = weight[:, tap * LANES : (tap + 1) * LANES]
                if flipped:
                    block = block.astype(F32).T.astype(BF16)
                for y in range(n_y):
                    lane = along_z * width + (y + along_y) * LANES
                    target[along_x, y * LANES : (y + 1) * LANES, lane : lane + LANES] = block


def down_weight(weight):
    channels = LANES // 2
    left = left_half((weight.shape[0], LANES))
    pieces = []
    for a in range(2):
        zero = weight[:, 4 * a * channels : 4 * a * channels + LANES].astype(F32)
        one = weight[:, (4 * a + 2) * channels : (4 * a + 2) * channels + LANES].astype(F32)
        pieces.append(jnp.where(left, zero, pltpu.roll(one, channels, 1)))
        pieces.append(jnp.where(left, pltpu.roll(zero, channels, 1), one))
    return jnp.concatenate(pieces, axis=1)


def up_weight(weight):
    pieces = []
    for a in range(2):
        for c in range(2):
            for b in range(2):
                tap = 4 * a + 2 * b + c
                pieces.append(weight[:, tap * LANES : (tap + 1) * LANES].astype(F32))
    return jnp.concatenate(pieces, axis=0)


def block_kernel(
    counts, field, cotan, weight_first, weight_last, weight_down, weight_coarse, weight_up,
    output, packed,
    field_w, cotan_w, summed_w, coarse_w, level_w, hidden, back_sum, back_first,
    shifted, shifted_c, w_first, w_last_t, w_last, w_coarse, w_coarse_t, twice,
    cells_ref, cells_f32, total_ref, send, recv,
):
    size = 2 * LANES
    channels = weight_first.shape[0]
    rows, lanes = field.shape
    n_x, n_y = lanes // size, rows // channels
    n_qx, n_qy = n_x // 2, n_y // 2
    width = n_qx * LANES
    fine_rows, coarse_rows = field_w.shape[0], coarse_w.shape[0]
    fine_rim, coarse_rim = (channels, size), (LANES, LANES)
    left = left_half((channels, LANES))
    n_cells = n_qx * n_qy * LANES

    for wide in (field_w, cotan_w, summed_w):
        clear_rim(counts, wide, fine_rim)
    for wide in (coarse_w, level_w):
        clear_rim(counts, wide, coarse_rim)
    matrix = parity_matrix(size, False)
    for source, wide in ((field, field_w), (cotan, cotan_w)):
        for x in range(n_x):
            wide[channels : channels + rows, (x + 1) * size : (x + 2) * size] = dot(
                source[:, x * size : (x + 1) * size], matrix
            ).astype(BF16)
    greet(counts)
    copies = [send_rim(counts, field_w, fine_rim, send, recv, 0)]
    copies.append(send_rim(counts, cotan_w, fine_rim, send, recv, 1))

    band_fine(weight_first, twice, w_first, n_y, False)
    band_fine(weight_last, twice, w_last_t, n_y, True)
    band_coarse(weight_coarse, w_coarse, n_qy, False)
    w_down = down_weight(weight_down)
    w_down_t = w_down.T.astype(BF16)
    w_down = w_down.astype(BF16)
    w_up = up_weight(weight_up)
    w_up_t = w_up.T.astype(BF16)
    w_up = w_up.astype(BF16)

    rim_arrived(counts, copies[0])
    fine_shifts(field_w, shifted)

    def store_hidden(where, value):
        hidden[:, where] = leaky(value).astype(BF16)

    fine_conv(shifted, w_first, store_hidden)
    for row, lane, fine_row, fine_lane in cells(n_qx, n_qy):
        cells_ref[part(row, lane)] = hidden[part(fine_row, fine_lane)]
    value = leaky(dot(w_down, cells_ref[...])).astype(BF16)
    for qy in range(n_qy):
        coarse_w[(qy + 1) * LANES : (qy + 2) * LANES, LANES : LANES + width] = value[:, qy * width : (qy + 1) * width]
    copies.append(send_rim(counts, coarse_w, coarse_rim, send, recv, 2))

    rim_arrived(counts, copies[1])
    fine_shifts(cotan_w, shifted)

    def store_back(where, value):
        back_sum[:, where] = value

    fine_conv(shifted, w_last_t, store_back)

    rim_arrived(counts, copies[2])
    coarse_shifts(coarse_w, shifted_c)
    level = to_wide(leaky(coarse_conv(shifted_c, w_coarse)).astype(BF16), n_qy, LANES)
    cells_f32[...] = dot(w_up, level)
    for row, lane, fine_row, fine_lane in cells(n_qx, n_qy):
        here, fine = part(row, lane), part(fine_row, fine_lane)
        value = cells_f32[here]
        root = lax.rsqrt(value * value + 1.0)
        summed_w[
            channels + fine_row * LANES : channels + (fine_row + 1) * LANES,
            size + fine_lane * LANES : size + (fine_lane + 1) * LANES,
        ] = (leaky(value) + hidden[fine].astype(F32)).astype(BF16)
        cells_ref[here] = (back_sum[fine] * (0.505 + 0.495 * value * root)).astype(BF16)
    back = (dot(w_up_t, cells_ref[...]) * slope_of(level)).astype(BF16)
    for qy in range(n_qy):
        level_w[(qy + 1) * LANES : (qy + 2) * LANES, LANES : LANES + width] = back[:, qy * width : (qy + 1) * width]
    copies.append(send_rim(counts, level_w, coarse_rim, send, recv, 3))
    copies.append(send_rim(counts, summed_w, fine_rim, send, recv, 4))

    packed[...] = jnp.zeros(packed.shape, BF16)
    base = 27 * channels + 27 * LANES
    packed[base : base + 8 * channels, :] = dot_nt(cells_ref[...], level).astype(BF16)
    base = 27 * channels
    center = level_w[LANES : LANES * (1 + n_qy), LANES : LANES + width]
    for along_x in range(3):
        total_ref[:, : 3 * coarse_rows] = dot_nt(center, shifted_c[:, along_x * LANES : along_x * LANES + width])
        for along_z in range(3):
            for along_y in range(3):
                term = None
                for qy in range(n_qy):
                    lane = along_z * coarse_rows + (qy + along_y) * LANES
                    here = total_ref[qy * LANES : (qy + 1) * LANES, lane : lane + LANES]
                    term = here if term is None else term + here
                at = base + (along_x * 9 + along_y * 3 + along_z) * LANES
                packed[at : at + LANES, :] = term.astype(BF16)
    band_coarse(weight_coarse, w_coarse_t, n_qy, True)
    band_fine(weight_last, twice, w_last, n_y, False)
    fine_shifts(field_w, shifted)

    rim_arrived(counts, copies[3])
    coarse_shifts(level_w, shifted_c)
    center = coarse_w[LANES : LANES * (1 + n_qy), LANES : LANES + width]
    back = to_wide((coarse_conv(shifted_c, w_coarse_t) * slope_of(center)).astype(BF16), n_qy, LANES)
    cells_f32[...] = dot(w_down_t, back)
    for row, lane, fine_row, fine_lane in cells(n_qx, n_qy):
        here, fine = part(row, lane), part(fine_row, fine_lane)
        mine = hidden[fine]
        cells_ref[here] = mine
        back_first[fine] = ((back_sum[fine] + cells_f32[here]) * slope_of(mine)).astype(BF16)
    base = 27 * channels + 27 * LANES + 8 * channels
    down = dot_nt(back, cells_ref[...])
    for k in range(4):
        packed[base + k * LANES : base + (k + 1) * LANES, :] = down[:, k * LANES : (k + 1) * LANES].astype(BF16)

    def weight_grad(value, second):
        for along_x in range(3):
            total_ref[:, : 3 * fine_rows] = dot_nt(value, shifted[:, along_x * size : along_x * size + lanes])
            for along_z in range(3):
                total = None
                for y in range(n_y):
                    term = total_ref[y * channels : (y + 1) * channels, along_z * fine_rows : (along_z + 1) * fine_rows]
                    if y > 0:
                        term = pltpu.roll(term, fine_rows - channels * y, 1)
                    term = term[:, : 2 * LANES]
                    total = term if total is None else total + term
                at = (along_x * 3 + along_z) * 3 * channels
                tail = at + 2 * channels
                head = total[:, :LANES].astype(BF16)
                rest = total[:, LANES:]
                if second:
                    packed[at + channels : at + 2 * channels, :] = head
                    rest = pltpu.roll(rest, channels, 1)
                    packed[tail : tail + channels, :] = jnp.where(
                        left, packed[tail : tail + channels, :].astype(F32), rest
                    ).astype(BF16)
                else:
                    packed[at : at + channels, :] = head
                    packed[tail : tail + channels, :] = rest.astype(BF16)

    weight_grad(back_first[...], False)
    rim_arrived(counts, copies[4])
    fine_shifts(summed_w, shifted)
    weight_grad(cotan_w[channels : channels + rows, size : size + lanes], True)
    matrix = parity_matrix(size, True)

    def store(where, value):
        output[:, where] = dot(value.astype(BF16), matrix).astype(BF16)

    fine_conv(shifted, w_last, store)
    for group in copies:
        rim_left(counts, group)


def unpack_kernel(sums, first, down, coarse, up, last):
    channels = first.shape[0]
    left = left_half((channels, LANES))

    def piece(tap, which, side):
        along_x, along_y, along_z = tap // 9, tap // 3 % 3, tap % 3
        at = (along_x * 3 + along_z) * 3 * channels
        at += 2 * channels if along_y == 2 else which * channels
        held = which if along_y == 2 else along_y
        value = sums[at : at + channels, :].astype(F32)
        return value if held == side else pltpu.roll(value, channels, 1)

    for which, target in ((0, first), (1, last)):
        for k in range(13):
            target[:, k * LANES : (k + 1) * LANES] = jnp.where(
                left, piece(2 * k, which, 0), piece(2 * k + 1, which, 1)
            )
        target[:, 13 * LANES : 13 * LANES + channels] = piece(26, which, 0)[:, :channels]
    at = 27 * channels
    for k in range(27):
        coarse[:, k * LANES : (k + 1) * LANES] = sums[at + k * LANES : at + (k + 1) * LANES, :].astype(F32)
    at += 27 * LANES
    for a in range(2):
        for c in range(2):
            for b in range(2):
                tap, row = 4 * a + 2 * b + c, at + (4 * a + 2 * c + b) * channels
                up[:, tap * LANES : (tap + 1) * LANES] = sums[row : row + channels, :].astype(F32)
    at += 8 * channels
    wide_left = left_half((LANES, LANES))
    for a in range(2):
        zero = sums[at + 2 * a * LANES : at + (2 * a + 1) * LANES, :].astype(F32)
        one = sums[at + (2 * a + 1) * LANES : at + (2 * a + 2) * LANES, :].astype(F32)
        base = 2 * a * LANES
        down[:, base : base + LANES] = jnp.where(wide_left, zero, pltpu.roll(one, channels, 1))
        down[:, base + LANES : base + 2 * LANES] = jnp.where(wide_left, pltpu.roll(zero, channels, 1), one)


def shards(counts, field, weight_first, weight_down, weight_coarse, weight_up, weight_last, cotangent):
    channels, size_x, size_y, size_z = field.shape
    wide = weight_down.shape[0]
    n_qx, n_qy = size_x // 2, size_y // 2
    rows, lanes = size_y * channels, size_x * size_z
    fine = lambda v: jnp.transpose(v, (2, 0, 1, 3)).reshape(rows, lanes)
    shape = jax.ShapeDtypeStruct

    whole = lambda v: jnp.pad(v, ((0, 0), (0, channels)))
    weight_first, weight_last = whole(weight_first), whole(weight_last)
    wide_rows, wide_lanes = (size_y + 2) * channels, (size_x + 2) * size_z
    coarse_rows, coarse_lanes = (n_qy + 2) * wide, (n_qx + 2) * LANES
    n_cells = n_qx * n_qy * LANES
    used = 27 * channels + 27 * wide + 8 * channels + 4 * wide
    devices = counts[0] * counts[1]
    chunk = -(-used // (devices * 16)) * 16
    output, packed = call(
        functools.partial(block_kernel, counts),
        [fine(field), fine(cotangent), weight_first, weight_last, weight_down, weight_coarse, weight_up],
        [shape((rows, lanes), BF16), shape((chunk * devices, LANES), BF16)],
        [pltpu.VMEM((wide_rows, wide_lanes), BF16)] * 3
        + [pltpu.VMEM((coarse_rows, coarse_lanes), BF16)] * 2
        + [
            pltpu.VMEM((rows, lanes), BF16),
            pltpu.VMEM((rows, lanes), F32),
            pltpu.VMEM((rows, lanes), BF16),
            pltpu.VMEM((3 * wide_rows, wide_lanes), BF16),
            pltpu.VMEM((3 * coarse_rows, coarse_lanes), BF16),
        ]
        + [pltpu.VMEM((3, rows, 3 * wide_rows), BF16)] * 3
        + [pltpu.VMEM((3, n_qy * wide, 3 * coarse_rows), BF16)] * 2
        + [
            pltpu.VMEM((27 * channels, LANES), F32),
            pltpu.VMEM((8 * channels, n_cells), BF16),
            pltpu.VMEM((8 * channels, n_cells), F32),
            pltpu.VMEM((max(rows, n_qy * wide), 3 * max(wide_rows, coarse_rows)), F32),
            pltpu.SemaphoreType.DMA((5, 8)),
            pltpu.SemaphoreType.DMA((5, 8)),
        ],
        "block",
        0,
    )
    first_part = -(-chunk // 32) * 16
    chunks = [size for size in (first_part, chunk - first_part) if size > 0]
    sums = sum_all(packed, chunks, counts, 3)
    grad_first, grad_down, grad_coarse, grad_up, grad_last = call(
        unpack_kernel,
        [sums],
        [
            shape((channels, 27 * channels), F32),
            shape((wide, 8 * channels), F32),
            shape((wide, 27 * wide), F32),
            shape((channels, 8 * wide), F32),
            shape((channels, 27 * channels), F32),
        ],
        [],
        "unpack",
    )
    output = jnp.transpose(output.reshape(size_y, channels, size_x, size_z), (1, 2, 0, 3))
    return (output, grad_first, grad_down, grad_coarse, grad_up, grad_last)


def solution(mesh):
    counts = (mesh.shape["gx"], mesh.shape["gy"])
    in_specs = (P(None, "gx", "gy", None), P(), P(), P(), P(), P(), P(None, "gx", "gy", None))
    out_specs = (P(None, "gx", "gy", None), P(), P(), P(), P(), P())
    return jax.shard_map(
        functools.partial(shards, counts), mesh=mesh, in_specs=in_specs, out_specs=out_specs, check_vma=False
    )
```
